32 devices in a mesh: space: 4 (over z), date: 8 (over y, x, core).
Axes of the slice: x: 2, y: 2, z: 4, core: 2. Of those that a mesh axis runs over, the one named last changes fastest.
Arguments:
- slc: bfloat16 [32, 128, 1024], P('date', 'space'), may hold values from -6 to 6
- footprint: int32 [128, 2], replicated, may hold values from -1 to 31, as said below
- valid_rows: int32 [4], P('space'), may hold values from 16 to 32
- pair_dates: int32 [528, 2], P('date'), may hold values from 0 to 31, as said below
Outputs:
- coherence: float32 [528, 4, 2, 8, 128], P('date', 'space')
The draws below stay inside these ranges and needn't reach their ends.
Inputs may be any that keep to these rules, and one draw needn't show every extreme that they name: `footprint`: column 0 names a tile, or -1 for a block outside every tile; column 1 a row of that tile (0 for -1). No two blocks share a tile row. At most 8 blocks held by one index of space go to one tile, and for every tile exactly 8 come from some one index. `pair_dates`: each row names two dates, the first no later than the second; every one of the 528 pairs stands in some row.
All inputs are finite; a program needn't handle non-finite values.
Results may differ from the reference program's by a relative error of at most 0.0019.
Values may be sent and summed in bfloat16 or wider, within the bound.
A program may use at most 64 MiB of HBM per device.

```python
import jax
import jax.numpy as jnp
import numpy as np
from jax import lax

DATES = 32
CAP = 8
TC = 512
TR = 32
NB_SRC = 32
SOURCES = 128
PAIRS = 528
SLOTS = 528
N_SPACE = 4


def draw_footprint(key, part):
    base = jax.random.fold_in(key, 7)
    key_count, key_top, key_rows, key_slots = jax.random.split(base, 4)
    counts = jax.random.randint(key_count, (N_SPACE, N_SPACE), 0, CAP + 1)
    top = jax.random.randint(key_top, (N_SPACE,), 0, N_SPACE)
    sources = jnp.arange(N_SPACE, dtype=jnp.int32)
    counts = jnp.where(sources[:, None] == top[None, :], CAP, counts).astype(jnp.int32)
    cum = jnp.cumsum(counts, axis=1)
    starts = cum - counts
    slot_ids = jnp.arange(NB_SRC, dtype=jnp.int32)
    tile_of = jnp.sum((slot_ids[None, :, None] >= cum[:, None, :]).astype(jnp.int32), axis=2)
    used = tile_of < N_SPACE
    safe = jnp.minimum(tile_of, N_SPACE - 1)
    within = slot_ids[None, :] - jnp.take_along_axis(starts, safe, axis=1)
    before = jnp.cumsum(counts, axis=0) - counts
    rank = jnp.take_along_axis(before, safe, axis=1) + within
    row_perm = jax.vmap(lambda k: jax.random.permutation(k, TR))(jax.random.split(key_rows, N_SPACE))
    rows = row_perm[safe, jnp.clip(rank, 0, TR - 1)]
    tiles = jnp.where(used, tile_of, -1)
    rows = jnp.where(used, rows, 0)
    slot_perm = jax.vmap(lambda k: jax.random.permutation(k, NB_SRC))(jax.random.split(key_slots, N_SPACE))
    tiles = jnp.take_along_axis(tiles, slot_perm, axis=1)
    rows = jnp.take_along_axis(rows, slot_perm, axis=1)
    return jnp.stack([tiles.reshape(-1), rows.reshape(-1)], axis=1).astype(jnp.int32)


def draw_pair_dates(key, part):
    order = jax.random.permutation(jax.random.fold_in(key, 3), SLOTS) % PAIRS
    firsts, seconds = np.triu_indices(DATES)
    table = jnp.asarray(np.stack([firsts, seconds], axis=1), dtype=jnp.int32)
    return table[order]


def plant(result, stream_key, least, top_value):
    index_at = [jax.random.randint(jax.random.fold_in(stream_key, axis), (), 0, length) for axis, length in enumerate(result.shape)]
    widest = result.shape.index(max(result.shape))
    neighbour = index_at[:widest] + [(index_at[widest] + 1) % result.shape[widest]] + index_at[widest + 1:]
    return result.at[tuple(index_at)].set(least).at[tuple(neighbour)].set(top_value)


def level_of(key, dims, cuts, least, largest):
    def one(position, shards_of):
        draws = jax.random.uniform(jax.random.fold_in(jax.random.fold_in(key, 6), position), (shards_of,), jnp.float32, least / len(cuts), largest / len(cuts))
        return jnp.repeat(jnp.exp(draws), dims[position] // shards_of).reshape((-1,) + (1,) * (len(dims) - position - 1))

    factor_of = one(*cuts[0])
    for cut in cuts[1:]:
        factor_of = factor_of * one(*cut)
    return factor_of


def scatter_about(stream_key, extent, spread, limit, cuts=(), kind=jnp.bfloat16):
    entries = jax.random.normal(stream_key, extent, jnp.float32) * spread
    if len(cuts) > 0:
        entries = level_of(stream_key, extent, cuts, -0.22, 0.18) * entries
    return jnp.clip(entries, min=-limit, max=limit).astype(kind)


def setup_inputs(seed: int = 0) -> dict:
    key_of = jax.random.split(jax.random.key(seed), 5)
    return {
        "slc": scatter_about(key_of[0], (DATES, SOURCES, 2 * TC), 1.0, 6.0, ((0, 8), (1, 4))),
        "footprint": draw_footprint(jax.random.fold_in(key_of[4], 71), 0),
        "valid_rows": plant(jax.random.randint(key_of[2], (N_SPACE,), TR // 2, TR + 1), jax.random.fold_in(key_of[2], 1), TR // 2, TR).astype(jnp.int32),
        "pair_dates": draw_pair_dates(jax.random.fold_in(key_of[4], 71), 0),
    }


def window_tables(rows, cols):
    row_out = jnp.arange(rows // 4, dtype=jnp.int32)[:, None]
    row_in = jnp.arange(rows, dtype=jnp.int32)[None, :]
    row_table = ((row_in >= 4 * row_out) & (row_in <= 4 * row_out + 4)).astype(jnp.float32)
    col_in = jnp.arange(cols, dtype=jnp.int32)[:, None]
    col_out = jnp.arange(cols // 4, dtype=jnp.int32)[None, :]
    col_table = (jnp.abs(col_in - 4 * col_out - 2) <= 5).astype(jnp.float32)
    return (row_table, col_table)

def reference(slc, footprint, valid_rows, pair_dates):
    high = lax.Precision.HIGHEST
    fp_tile = footprint[:, 0]
    fp_row = footprint[:, 1]
    target = jnp.where(fp_tile < 0, N_SPACE, fp_tile).astype(jnp.int32)
    placed = jnp.zeros((DATES, N_SPACE + 1, TR, 2 * TC), slc.dtype)
    placed = placed.at[:, target, fp_row].set(slc)[:, :N_SPACE]
    keep = jnp.arange(TR, dtype=jnp.int32)[None, :] < valid_rows[:, None]
    tiles = jnp.where(keep[None, :, :, None], placed, jnp.zeros_like(placed))
    tiles = tiles.reshape(DATES, N_SPACE, TR, 2, TC)
    row_table, col_table = window_tables(TR, TC)
    real = tiles[:, :, :, 0].astype(jnp.float32)
    imag = tiles[:, :, :, 1].astype(jnp.float32)
    power = (real * real + imag * imag).astype(jnp.bfloat16).astype(jnp.float32)
    colsum = jnp.einsum('dsrw,wk->dsrk', power, col_table, precision=high)
    looked = jnp.einsum('mr,dsrk->dsmk', row_table, colsum, precision=high)
    floor = jnp.maximum(looked, 1.0)

    def one_slot(pair):
        first = tiles[pair[0]]
        second = tiles[pair[1]]
        real_a = first[:, :, 0].astype(jnp.float32)
        imag_a = first[:, :, 1].astype(jnp.float32)
        real_b = second[:, :, 0].astype(jnp.float32)
        imag_b = second[:, :, 1].astype(jnp.float32)
        cross_real = (real_a * real_b + imag_a * imag_b).astype(jnp.bfloat16)
        cross_imag = (imag_a * real_b - real_a * imag_b).astype(jnp.bfloat16)
        cross = jnp.stack([cross_real, cross_imag], axis=2).astype(jnp.float32)
        summed = jnp.einsum('srxw,wk->srxk', cross, col_table, precision=high)
        multi = jnp.einsum('mr,srxk->sxmk', row_table, summed, precision=high)
        scale = jnp.sqrt(floor[pair[0]] * floor[pair[1]])
        return multi / scale[:, None]
    return lax.map(one_slot, pair_dates)
```

```python
import functools

import jax
import jax.numpy as jnp
from jax import lax
from jax.experimental import pallas as pl
from jax.experimental.pallas import tpu as pltpu
from jax.sharding import PartitionSpec as P

CHUNKS = 4
Z_AHEAD = 2
MESH = pl.DeviceIdType.MESH
F32, BF16 = jnp.float32, jnp.bfloat16


def largest_divisor(count, most):
    return max(g for g in range(1, most + 1) if count % g == 0)


def partners(date, n_date):
    chips = n_date // 2
    chip, core = date // 2, date % 2
    sibling = chip * 2 + (1 - core)
    if chips == 4:
        x, y = chip % 2, chip // 2
        x1, y1 = core * x + (1 - core) * (1 - x), core * (1 - y) + (1 - core) * y
        x2, y2 = core * (1 - x) + (1 - core) * x, core * y + (1 - core) * (1 - y)
        others = [(y1 * 2 + x1) * 2 + core, (y2 * 2 + x2) * 2 + core, ((1 - y) * 2 + (1 - x)) * 2 + core]
        return sibling, others, others, True
    targets = [lax.rem(chip + k, chips) * 2 + core for k in range(1, chips)]
    sources = [lax.rem(chip + chips - k, chips) * 2 + core for k in range(1, chips)]
    return sibling, targets, sources, False


def tables(cfg, foot, valid, own):
    groups, n_date, dates_dev, blocks, width, cap, slots = cfg
    total, looks, lane = groups * blocks, blocks // 4, 128
    tile, row = foot[0:1], foot[1:2]

    def index(shape, dim):
        return lax.broadcasted_iota(jnp.int32, shape, dim)

    def ones(mask):
        return mask.astype(F32).astype(BF16)

    earlier = (index((lane, lane), 0) < index((lane, lane), 1)) & (
        lax.div(index((lane, lane), 0), blocks) == lax.div(index((lane, lane), 1), blocks)
    )
    ranks = []
    for at in range(0, total, lane):
        hot = index((max(groups, 8), lane), 0) == tile[:, at : at + lane]
        count = jnp.dot(ones(hot), ones(earlier), preferred_element_type=F32)
        ranks.append(jnp.sum(jnp.where(hot, count, 0.0), axis=0, keepdims=True))
    rank = jnp.concatenate(ranks, axis=1).astype(jnp.int32)

    n_slot, n_place = groups * dates_dev * cap, dates_dev * blocks
    slot = index((n_slot, total), 0)
    slot_group, slot_rank = lax.div(slot, dates_dev * cap), lax.rem(slot, cap)
    slot_date = lax.rem(lax.div(index((n_slot, n_place), 0), cap), dates_dev)
    fits = slot_rank == rank
    leaves = ones(fits & (slot_group == tile))
    held = ones(index((total, n_place), 0) == own * blocks + lax.rem(index((total, n_place), 1), blocks))
    select = jnp.dot(leaves, held, preferred_element_type=F32)
    select = jnp.where(slot_date == lax.div(index((n_slot, n_place), 1), blocks), select, 0.0)

    place_at = lax.rem(row, 4) * looks + lax.div(row, 4)
    place_at = jnp.where((tile == own) & (row < valid), place_at, -1)
    lands = ones(lax.rem(index((n_place, total), 0), blocks) == place_at)
    comes = ones(fits & (slot_group == lax.div(index((n_slot, total), 1), blocks)))
    place = lax.dot_general(lands, comes, (((1,), (1,)), ((), ())), preferred_element_type=F32)
    from_date = lax.rem(lax.div(index((n_place, n_slot), 1), cap), dates_dev)
    place = jnp.where(from_date == lax.div(index((n_place, n_slot), 0), blocks), place, 0.0)
    return select.astype(BF16), place.astype(BF16)


def kernel(cfg, slc_hbm, foot_hbm, valid_ref, pairs_hbm, out_ref, *scratch):
    groups, n_date, dates_dev, blocks, width, cap, slots = cfg
    out_bufs, in_bufs = scratch[:CHUNKS], scratch[CHUNKS : 2 * CHUNKS]
    panels = scratch[2 * CHUNKS : 3 * CHUNKS]
    rest = scratch[3 * CHUNKS :]
    floor_ref, z_send, z_recv, d_send, d_recv, f_send, f_recv, c_send, c_recv = rest[:9]
    slc_ref, foot_ref, pairs_ref, in_sem = rest[9:]
    wc = width // CHUNKS
    looks = blocks // 4
    dates = n_date * dates_dev
    own, date = lax.axis_index("space"), lax.axis_index("date")
    sibling, targets, sources, corner = partners(date, n_date)
    direct = targets[:2] if corner else targets
    peers = [lax.rem(own + k, groups) for k in range(1, groups)]

    barrier = pltpu.get_barrier_semaphore()
    for peer in peers:
        pl.semaphore_signal(barrier, inc=1, device_id={"space": peer}, device_id_type=MESH)
    for target in direct + [sibling]:
        pl.semaphore_signal(barrier, inc=1, device_id={"date": target}, device_id_type=MESH)

    fetches = [
        pltpu.make_async_copy(src, dst, in_sem.at[k])
        for k, (src, dst) in enumerate([(foot_hbm, foot_ref), (slc_hbm, slc_ref), (pairs_hbm, pairs_ref)])
    ]
    for fetch in fetches:
        fetch.start()
    fetches[0].wait()
    select, place = tables(cfg, foot_ref[...], valid_ref[0], own)
    fetches[1].wait()
    fetches[2].wait()

    def gather_rows(c):
        for part in range(2):
            cols = slice(part * width + c * wc, part * width + (c + 1) * wc)
            rows = jnp.dot(select, slc_ref[:, cols], preferred_element_type=F32).astype(BF16)
            out_bufs[c][:, :, part * wc : (part + 1) * wc] = rows.reshape(groups, dates_dev * cap, wc)

    sends = []

    def z_copy(c, k):
        return pltpu.make_async_remote_copy(
            src_ref=out_bufs[c].at[peers[k]],
            dst_ref=in_bufs[c].at[own],
            send_sem=z_send.at[c, k],
            recv_sem=z_recv.at[c, k],
            device_id={"space": peers[k]},
            device_id_type=MESH,
        )

    def panel_copy(c, source, target, send_sem, recv_sem):
        block = panels[c].at[pl.ds(source * dates_dev, dates_dev)]
        return pltpu.make_async_remote_copy(
            src_ref=block,
            dst_ref=block,
            send_sem=send_sem,
            recv_sem=recv_sem,
            device_id={"date": target},
            device_id_type=MESH,
        )

    z_copies, d_copies, s_copies, r_copies = {}, {}, {}, {}

    def stage_send(c):
        gather_rows(c)
        if c == 0:
            pl.semaphore_wait(barrier, len(peers) + len(direct) + 1)
        for k in range(len(peers)):
            z_copies[c, k] = z_copy(c, k)
            if c < Z_AHEAD:
                z_copies[c, k].start()
        in_bufs[c][own] = out_bufs[c][own]

    def stage_place(c):
        for k in range(len(peers)):
            z_copies[c, k].wait_recv()
            if c + Z_AHEAD < CHUNKS:
                z_copies[c, k].wait_send()
                z_copies[c + Z_AHEAD, k].start()
        rows = in_bufs[c][...].reshape(groups * dates_dev * cap, 2 * wc)
        tile = jnp.dot(place, rows, preferred_element_type=F32).astype(BF16)
        panels[c][pl.ds(date * dates_dev, dates_dev)] = tile.reshape(dates_dev, blocks, 2 * wc)
        for k, target in enumerate(direct):
            d_copies[c, k] = panel_copy(c, date, target, d_send.at[c, k], d_recv.at[c, k])
            d_copies[c, k].start()
        s_copies[c] = panel_copy(c, date, sibling, c_send.at[c], c_recv.at[c])
        s_copies[c].start()

    def to_sibling(c, k):
        r_copies[c, k] = panel_copy(c, sources[k], sibling, f_send.at[c, k], f_recv.at[c, k])
        r_copies[c, k].start()

    def stage_forward(c):
        for k in range(len(direct)):
            if corner and k == 1:
                continue
            d_copies[c, k].wait_recv()
            if corner and k == 0:
                d_copies[c, 2] = panel_copy(c, sources[0], targets[1], d_send.at[c, 2], d_recv.at[c, 2])
                d_copies[c, 2].start()
            to_sibling(c, k)

    def stage_corner(c):
        if corner:
            d_copies[c, 1].wait_recv()
            to_sibling(c, 1)
            d_copies[c, 2].wait_recv()
            to_sibling(c, 2)

    def row_sum(summed, count):
        quads = summed.reshape(count, 4, looks, 128)
        last = lax.broadcasted_iota(jnp.int32, (count, looks, 128), 1) == looks - 1
        below = jnp.where(last, 0.0, pltpu.roll(quads[:, 0], looks - 1, 1))
        return quads[:, 0] + quads[:, 1] + quads[:, 2] + quads[:, 3] + below

    def stage_looks(c):
        s_copies[c].wait_recv()
        for k in range(len(sources)):
            r_copies[c, k].wait_recv()
        panel = panels[c]
        col_in = lax.broadcasted_iota(jnp.int32, (wc, 128), 0) + c * wc
        col_out = lax.broadcasted_iota(jnp.int32, (wc, 128), 1)
        table = (jnp.abs(col_in - 4 * col_out - 2) <= 5).astype(F32).astype(BF16)
        last = c == CHUNKS - 1

        group = largest_divisor(dates, max(1, 256 // blocks))

        def power_body(n, carry):
            rows = panel[pl.ds(n * group, group)].astype(F32)
            real, imag = rows[:, :, :wc], rows[:, :, wc:]
            power = (real * real + imag * imag).astype(BF16).reshape(group * blocks, wc)
            looked = row_sum(jnp.dot(power, table, preferred_element_type=F32), group)
            at = pl.ds(n * group, group)
            if c > 0:
                looked = looked + floor_ref[at]
            if last:
                looked = lax.rsqrt(jnp.maximum(looked, 1.0))
            floor_ref[at] = looked
            return carry

        lax.fori_loop(0, dates // group, power_body, 0, unroll=True)

        batch = largest_divisor(slots, max(1, 352 // blocks))

        def pair_body(n, carry):
            crosses, scales = [], []
            for g in range(batch):
                p = n * batch + g
                i, j = pairs_ref[0, p], pairs_ref[1, p]
                first, second = panel[i].astype(F32), panel[j].astype(F32)
                ra, ia, rb, ib = first[:, :wc], first[:, wc:], second[:, :wc], second[:, wc:]
                crosses.append((ra * rb + ia * ib).astype(BF16))
                crosses.append((ia * rb - ra * ib).astype(BF16))
                if last:
                    scales.append(floor_ref[i] * floor_ref[j])
            cross = jnp.concatenate(crosses, axis=0)
            looked = row_sum(jnp.dot(cross, table, preferred_element_type=F32), 2 * batch)
            looked = looked.reshape(batch, 2, looks, 128)
            at = pl.ds(n * batch, batch)
            if c > 0:
                looked = looked + out_ref[at]
            if last:
                looked = looked * jnp.stack(scales)[:, None]
            out_ref[at] = looked
            return carry

        lax.fori_loop(0, slots // batch, pair_body, 0, unroll=True)

    for step in range(CHUNKS):
        stage_send(step)
    for step in range(CHUNKS + 3):
        for lag, stage in enumerate((stage_place, stage_forward, stage_corner, stage_looks)):
            if 0 <= step - lag < CHUNKS:
                stage(step - lag)
    for copies in (z_copies, d_copies, s_copies, r_copies):
        for at, copy in copies.items():
            if copies is not z_copies or at[0] + Z_AHEAD >= CHUNKS:
                copy.wait_send()


def on_device(slc, footprint, valid_rows, pair_dates):
    groups, n_date = lax.axis_size("space"), lax.axis_size("date")
    dates_dev, blocks, twice = slc.shape
    width = twice // 2
    cap = blocks // groups
    slots = pair_dates.shape[0]
    looks = blocks // 4
    wc = width // CHUNKS
    others = n_date // 2 - 1
    sem = pltpu.SemaphoreType.DMA
    cfg = (groups, n_date, dates_dev, blocks, width, cap, slots)
    far = functools.partial(pltpu.with_memory_space_constraint, memory_space=pltpu.HBM)
    hbm, smem = pl.BlockSpec(memory_space=pltpu.HBM), pl.BlockSpec(memory_space=pltpu.SMEM)
    result = pl.pallas_call(
        functools.partial(kernel, cfg),
        out_shape=jax.ShapeDtypeStruct((slots, 2, looks, 128), F32),
        in_specs=[hbm, hbm, smem, hbm],
        out_specs=pl.BlockSpec(memory_space=pltpu.VMEM),
        scratch_shapes=[pltpu.VMEM((groups, dates_dev * cap, 2 * wc), BF16)] * (2 * CHUNKS)
        + [pltpu.VMEM((n_date * dates_dev, blocks, 2 * wc), BF16)] * CHUNKS
        + [
            pltpu.VMEM((n_date * dates_dev, looks, 128), F32),
            sem((CHUNKS, groups - 1)),
            sem((CHUNKS, groups - 1)),
            sem((CHUNKS, others)),
            sem((CHUNKS, others)),
            sem((CHUNKS, others)),
            sem((CHUNKS, others)),
            sem((CHUNKS,)),
            sem((CHUNKS,)),
            pltpu.VMEM((dates_dev * blocks, twice), BF16),
            pltpu.VMEM(footprint.shape[::-1], jnp.int32),
            pltpu.SMEM(pair_dates.shape[::-1], jnp.int32),
            sem((3,)),
        ],
        compiler_params=pltpu.CompilerParams(
            collective_id=0, has_side_effects=True, vmem_limit_bytes=40 * 1024 * 1024
        ),
    )(far(slc.reshape(dates_dev * blocks, twice)), far(footprint.T), valid_rows, far(pair_dates.T))
    return result[:, None]


def solution(mesh):
    in_specs = (P("date", "space", None), P(), P("space"), P("date", None))
    out_specs = P("date", "space", None, None, None)
    return jax.shard_map(
        on_device, mesh=mesh, in_specs=in_specs, out_specs=out_specs, check_vma=False
    )
```

```python
import functools

import jax
import jax.numpy as jnp
from jax import lax
from jax.experimental import pallas as pl
from jax.experimental.pallas import tpu as pltpu
from jax.sharding import PartitionSpec as P

WIDTHS = (1, 2, 1)
CHUNKS = len(WIDTHS)
RELAYED = ((False, False, False), (False, False, False))
ORDER = (('z', 0), ('z', 1), ('z', 2), ('e', 0), ('e', 1), ('e', 2), ('o', 0), ('o', 1), ('o', 2), ('f', 0), ('f', 1), ('c', 0), ('c', 1), ('l', 0), ('f', 2), ('c', 2), ('l', 1), ('l', 2))
MESH = pl.DeviceIdType.MESH
F32, BF16 = jnp.float32, jnp.bfloat16


def largest_divisor(count, most):
    return max(g for g in range(1, most + 1) if count % g == 0)


def partners(date, n_date):
    chips = n_date // 2
    chip, core = date // 2, date % 2
    sibling = chip * 2 + (1 - core)
    if chips == 4:
        x, y = chip % 2, chip // 2
        x1, y1 = core * x + (1 - core) * (1 - x), core * (1 - y) + (1 - core) * y
        x2, y2 = core * (1 - x) + (1 - core) * x, core * y + (1 - core) * (1 - y)
        others = [(y1 * 2 + x1) * 2 + core, (y2 * 2 + x2) * 2 + core, ((1 - y) * 2 + (1 - x)) * 2 + core]
        return sibling, others, others, True
    targets = [lax.rem(chip + k, chips) * 2 + core for k in range(1, chips)]
    sources = [lax.rem(chip + chips - k, chips) * 2 + core for k in range(1, chips)]
    return sibling, targets, sources, False


def tables(cfg, foot, valid, own):
    groups, n_date, dates_dev, blocks, width, cap, slots = cfg
    total, looks, lane = groups * blocks, blocks // 4, 128
    tile, row = foot[0:1], foot[1:2]
    tile_step = jnp.where(tile < 0, -1, lax.rem(tile - own + groups, groups))

    def index(shape, dim):
        return lax.broadcasted_iota(jnp.int32, shape, dim)

    def ones(mask):
        return mask.astype(F32).astype(BF16)

    earlier = (index((lane, lane), 0) < index((lane, lane), 1)) & (
        lax.div(index((lane, lane), 0), blocks) == lax.div(index((lane, lane), 1), blocks)
    )
    ranks = []
    for at in range(0, total, lane):
        hot = index((max(groups, 8), lane), 0) == tile[:, at : at + lane]
        count = jnp.dot(ones(hot), ones(earlier), preferred_element_type=F32)
        ranks.append(jnp.sum(jnp.where(hot, count, 0.0), axis=0, keepdims=True))
    rank = jnp.concatenate(ranks, axis=1).astype(jnp.int32)

    n_slot, n_place = groups * dates_dev * cap, dates_dev * blocks
    slot = index((n_slot, total), 0)
    slot_group, slot_rank = lax.div(slot, dates_dev * cap), lax.rem(slot, cap)
    slot_date = lax.rem(lax.div(index((n_slot, n_place), 0), cap), dates_dev)
    fits = slot_rank == rank
    leaves = ones(fits & (slot_group == tile_step))
    held = ones(index((total, n_place), 0) == own * blocks + lax.rem(index((total, n_place), 1), blocks))
    select = jnp.dot(leaves, held, preferred_element_type=F32)
    select = jnp.where(slot_date == lax.div(index((n_slot, n_place), 1), blocks), select, 0.0)

    place_at = lax.rem(row, 4) * looks + lax.div(row, 4)
    place_at = jnp.where((tile == own) & (row < valid), place_at, -1)
    lands = ones(lax.rem(index((n_place, total), 0), blocks) == place_at)
    from_step = lax.rem(lax.div(index((n_slot, total), 1), blocks) - own + groups, groups)
    comes = ones(fits & (slot_group == from_step))
    place = lax.dot_general(lands, comes, (((1,), (1,)), ((), ())), preferred_element_type=F32)
    from_date = lax.rem(lax.div(index((n_place, n_slot), 1), cap), dates_dev)
    place = jnp.where(from_date == lax.div(index((n_place, n_slot), 0), blocks), place, 0.0)
    return select.astype(BF16), place.astype(BF16)


def kernel(cfg, slc_hbm, foot_hbm, valid_ref, pairs_hbm, out_ref, *scratch):
    groups, n_date, dates_dev, blocks, width, cap, slots = cfg
    out_bufs, slot_bufs = scratch[:CHUNKS], scratch[CHUNKS : 2 * CHUNKS]
    panels = scratch[2 * CHUNKS : 3 * CHUNKS]
    rest = scratch[3 * CHUNKS :]
    floor_ref, z_send, z_recv, d_send, d_recv, f_send, f_recv, c_send, c_recv = rest[:9]
    slc_ref, foot_ref, pairs_ref, in_sem = rest[9:]
    looks = blocks // 4
    dates = n_date * dates_dev
    own, date = lax.axis_index("space"), lax.axis_index("date")
    sibling, targets, sources, corner = partners(date, n_date)
    peers = [lax.rem(own + k, groups) for k in range(1, groups)]

    wide = [width * w // sum(WIDTHS) for w in WIDTHS]
    left = [sum(wide[:c]) for c in range(CHUNKS)]

    barrier = pltpu.get_barrier_semaphore()
    for peer in peers:
        pl.semaphore_signal(barrier, inc=1, device_id={"space": peer}, device_id_type=MESH)
    for target in targets + [sibling]:
        pl.semaphore_signal(barrier, inc=1, device_id={"date": target}, device_id_type=MESH)

    fetches = [
        pltpu.make_async_copy(src, dst, in_sem.at[k])
        for k, (src, dst) in enumerate([(foot_hbm, foot_ref), (slc_hbm, slc_ref), (pairs_hbm, pairs_ref)])
    ]
    for fetch in fetches:
        fetch.start()
    fetches[0].wait()
    select, place = tables(cfg, foot_ref[...], valid_ref[0], own)
    fetches[1].wait()
    fetches[2].wait()

    def gather_rows(c):
        wc = wide[c]
        for part in range(2):
            cols = slice(part * width + left[c], part * width + left[c] + wc)
            half = slice(part * wc, (part + 1) * wc)
            rows = jnp.dot(select, slc_ref[:, cols], preferred_element_type=F32).astype(BF16)
            rows = rows.reshape(groups, dates_dev * cap, wc)
            slot_bufs[c][date, 0, :, half] = rows[0]
            out_bufs[c][:, :, half] = rows[1:]

    def z_copy(c, k):
        return pltpu.make_async_remote_copy(
            src_ref=out_bufs[c].at[k],
            dst_ref=slot_bufs[c].at[date, groups - 1 - k],
            send_sem=z_send.at[c, k],
            recv_sem=z_recv.at[c, k],
            device_id={"space": peers[k]},
            device_id_type=MESH,
        )

    def slot_copy(c, part, source, target, send_sem, recv_sem):
        steps = pl.ds(0, 1) if part == 0 else pl.ds(1, groups - 1)
        block = slot_bufs[c].at[source, steps]
        return pltpu.make_async_remote_copy(
            src_ref=block,
            dst_ref=block,
            send_sem=send_sem,
            recv_sem=recv_sem,
            device_id={"date": target},
            device_id_type=MESH,
        )

    z_copies, d_copies, s_copies, r_copies = {}, {}, {}, {}

    def relayed(c, part):
        return corner and RELAYED[part][c]

    def send(c, part):
        for k, target in enumerate(targets[:2] if relayed(c, part) else targets):
            d_copies[c, part, k] = slot_copy(c, part, date, target, d_send.at[c, part, k], d_recv.at[c, part, k])
            d_copies[c, part, k].start()

    def panel_copy(c, source, send_sem, recv_sem):
        block = panels[c].at[pl.ds(source * dates_dev, dates_dev)]
        return pltpu.make_async_remote_copy(
            src_ref=block,
            dst_ref=block,
            send_sem=send_sem,
            recv_sem=recv_sem,
            device_id={"date": sibling},
            device_id_type=MESH,
        )

    def fill(c, source):
        wc = wide[c]
        rows = slot_bufs[c][source].reshape(groups * dates_dev * cap, 2 * wc)
        tile = jnp.dot(place, rows, preferred_element_type=F32).astype(BF16)
        panels[c][pl.ds(source * dates_dev, dates_dev)] = tile.reshape(dates_dev, blocks, 2 * wc)

    def arrive(c, part, k):
        d_copies[c, part, k].wait_recv()
        if k == 0 and relayed(c, part):
            relay = slot_copy(c, part, sources[0], targets[1], d_send.at[c, part, 2], d_recv.at[c, part, 2])
            d_copies[c, part, 2] = relay
            relay.start()

    def to_sibling(c, k):
        arrive(c, 1, k)
        fill(c, sources[k])
        r_copies[c, k] = panel_copy(c, sources[k], f_send.at[c, k], f_recv.at[c, k])
        r_copies[c, k].start()

    def stage_send(c):
        gather_rows(c)
        if c == 0:
            pl.semaphore_wait(barrier, len(peers) + len(targets) + 1)
        for k in range(len(peers)):
            z_copies[c, k] = z_copy(c, k)
            z_copies[c, k].start()
        send(c, 0)

    def stage_z(c):
        for k in range(len(peers)):
            z_copies[c, k].wait_recv()
        send(c, 1)

    def stage_own(c):
        fill(c, date)
        s_copies[c] = panel_copy(c, date, c_send.at[c], c_recv.at[c])
        s_copies[c].start()

    def stage_early(c):
        for k in range(len(sources)):
            arrive(c, 0, k)

    def stage_forward(c):
        for k in range(1 if relayed(c, 1) else len(sources)):
            to_sibling(c, k)

    def stage_corner(c):
        if relayed(c, 1):
            to_sibling(c, 1)
            to_sibling(c, 2)

    def row_sum(summed, count):
        quads = summed.reshape(count, 4, looks, 128)
        last = lax.broadcasted_iota(jnp.int32, (count, looks, 128), 1) == looks - 1
        below = jnp.where(last, 0.0, pltpu.roll(quads[:, 0], looks - 1, 1))
        return quads[:, 0] + quads[:, 1] + quads[:, 2] + quads[:, 3] + below

    def stage_looks(c):
        s_copies[c].wait_recv()
        for k in range(len(sources)):
            r_copies[c, k].wait_recv()
        panel, wc = panels[c], wide[c]
        col_in = lax.broadcasted_iota(jnp.int32, (wc, 128), 0) + left[c]
        col_out = lax.broadcasted_iota(jnp.int32, (wc, 128), 1)
        table = (jnp.abs(col_in - 4 * col_out - 2) <= 5).astype(F32).astype(BF16)
        last = c == CHUNKS - 1

        group = largest_divisor(dates, max(1, 256 // blocks))

        def power_body(n, carry):
            rows = panel[pl.ds(n * group, group)].astype(F32)
            real, imag = rows[:, :, :wc], rows[:, :, wc:]
            power = (real * real + imag * imag).astype(BF16).reshape(group * blocks, wc)
            looked = row_sum(jnp.dot(power, table, preferred_element_type=F32), group)
            at = pl.ds(n * group, group)
            if c > 0:
                looked = looked + floor_ref[at]
            if last:
                looked = lax.rsqrt(jnp.maximum(looked, 1.0))
            floor_ref[at] = looked
            return carry

        lax.fori_loop(0, dates // group, power_body, 0, unroll=True)

        batch = largest_divisor(slots, max(1, 352 // blocks))

        def pair_body(n, carry):
            crosses, scales = [], []
            for g in range(batch):
                p = n * batch + g
                i, j = pairs_ref[0, p], pairs_ref[1, p]
                first, second = panel[i].astype(F32), panel[j].astype(F32)
                ra, ia, rb, ib = first[:, :wc], first[:, wc:], second[:, :wc], second[:, wc:]
                crosses.append((ra * rb + ia * ib).astype(BF16))
                crosses.append((ia * rb - ra * ib).astype(BF16))
                if last:
                    scales.append(floor_ref[i] * floor_ref[j])
            cross = jnp.concatenate(crosses, axis=0)
            looked = row_sum(jnp.dot(cross, table, preferred_element_type=F32), 2 * batch)
            looked = looked.reshape(batch, 2, looks, 128)
            at = pl.ds(n * batch, batch)
            if c > 0:
                looked = looked + out_ref[at]
            if last:
                looked = looked * jnp.stack(scales)[:, None]
            out_ref[at] = looked
            return carry

        lax.fori_loop(0, slots // batch, pair_body, 0, unroll=True)

    for c in range(CHUNKS):
        stage_send(c)
    stages = {
        "z": stage_z,
        "o": stage_own,
        "e": stage_early,
        "f": stage_forward,
        "c": stage_corner,
        "l": stage_looks,
    }
    for name, c in ORDER:
        stages[name](c)
    for copies in (z_copies, d_copies, s_copies, r_copies):
        for copy in copies.values():
            copy.wait_send()


def on_device(slc, footprint, valid_rows, pair_dates):
    groups, n_date = lax.axis_size("space"), lax.axis_size("date")
    dates_dev, blocks, twice = slc.shape
    width = twice // 2
    cap = blocks // groups
    slots = pair_dates.shape[0]
    looks = blocks // 4
    wide = [width * w // sum(WIDTHS) for w in WIDTHS]
    others = n_date // 2 - 1
    sem = pltpu.SemaphoreType.DMA
    cfg = (groups, n_date, dates_dev, blocks, width, cap, slots)
    far = functools.partial(pltpu.with_memory_space_constraint, memory_space=pltpu.HBM)
    hbm, smem = pl.BlockSpec(memory_space=pltpu.HBM), pl.BlockSpec(memory_space=pltpu.SMEM)
    result = pl.pallas_call(
        functools.partial(kernel, cfg),
        out_shape=jax.ShapeDtypeStruct((slots, 2, looks, 128), F32),
        in_specs=[hbm, hbm, smem, hbm],
        out_specs=pl.BlockSpec(memory_space=pltpu.VMEM),
        scratch_shapes=[pltpu.VMEM((groups - 1, dates_dev * cap, 2 * wc), BF16) for wc in wide]
        + [pltpu.VMEM((n_date, groups, dates_dev * cap, 2 * wc), BF16) for wc in wide]
        + [pltpu.VMEM((n_date * dates_dev, blocks, 2 * wc), BF16) for wc in wide]
        + [
            pltpu.VMEM((n_date * dates_dev, looks, 128), F32),
            sem((CHUNKS, groups - 1)),
            sem((CHUNKS, groups - 1)),
            sem((CHUNKS, 2, others)),
            sem((CHUNKS, 2, others)),
            sem((CHUNKS, others)),
            sem((CHUNKS, others)),
            sem((CHUNKS,)),
            sem((CHUNKS,)),
            pltpu.VMEM((dates_dev * blocks, twice), BF16),
            pltpu.VMEM(footprint.shape[::-1], jnp.int32),
            pltpu.SMEM(pair_dates.shape[::-1], jnp.int32),
            sem((3,)),
        ],
        compiler_params=pltpu.CompilerParams(
            collective_id=0, has_side_effects=True, vmem_limit_bytes=40 * 1024 * 1024
        ),
    )(far(slc.reshape(dates_dev * blocks, twice)), far(footprint.T), valid_rows, far(pair_dates.T))
    return result[:, None]


def solution(mesh):
    in_specs = (P("date", "space", None), P(), P("space"), P("date", None))
    out_specs = P("date", "space", None, None, None)
    return jax.shard_map(
        on_device, mesh=mesh, in_specs=in_specs, out_specs=out_specs, check_vma=False
    )
```

```python
import functools

import jax
import jax.numpy as jnp
from jax import lax
from jax.experimental import pallas as pl
from jax.experimental.pallas import tpu as pltpu
from jax.sharding import PartitionSpec as P

CHUNKS = 4
BATCH_ROWS, GROUP_ROWS = 1056, 1024
MESH = pl.DeviceIdType.MESH
F32, BF16 = jnp.float32, jnp.bfloat16


def largest_divisor(count, most):
    return max(g for g in range(1, most + 1) if count % g == 0)


def partners(date, n_date):
    chips = n_date // 2
    chip, core = date // 2, date % 2
    sibling = chip * 2 + (1 - core)
    targets = [lax.rem(chip + k, chips) * 2 + core for k in range(1, chips)]
    sources = [lax.rem(chip + chips - k, chips) * 2 + core for k in range(1, chips)]
    return sibling, targets, sources


def tables(cfg, foot, valid, own):
    groups, n_date, dates_dev, blocks, width, cap, slots = cfg
    total, looks, lane = groups * blocks, blocks // 4, 128
    tile, row = foot[0:1], foot[1:2]
    tile_step = jnp.where(tile < 0, -1, lax.rem(tile - own + groups, groups))

    def index(shape, dim):
        return lax.broadcasted_iota(jnp.int32, shape, dim)

    def ones(mask):
        return mask.astype(F32).astype(BF16)

    earlier = (index((lane, lane), 0) < index((lane, lane), 1)) & (
        lax.div(index((lane, lane), 0), blocks) == lax.div(index((lane, lane), 1), blocks)
    )
    ranks = []
    for at in range(0, total, lane):
        hot = index((max(groups, 8), lane), 0) == tile[:, at : at + lane]
        count = jnp.dot(ones(hot), ones(earlier), preferred_element_type=F32)
        ranks.append(jnp.sum(jnp.where(hot, count, 0.0), axis=0, keepdims=True))
    rank = jnp.concatenate(ranks, axis=1).astype(jnp.int32)

    n_slot, n_place = groups * dates_dev * cap, dates_dev * blocks
    slot = index((n_slot, total), 0)
    slot_group, slot_rank = lax.div(slot, dates_dev * cap), lax.rem(slot, cap)
    slot_date = lax.rem(lax.div(index((n_slot, n_place), 0), cap), dates_dev)
    fits = slot_rank == rank
    leaves = ones(fits & (slot_group == tile_step))
    held = ones(index((total, n_place), 0) == own * blocks + lax.rem(index((total, n_place), 1), blocks))
    select = jnp.dot(leaves, held, preferred_element_type=F32)
    select = jnp.where(slot_date == lax.div(index((n_slot, n_place), 1), blocks), select, 0.0)

    place_at = lax.rem(row, 4) * looks + lax.div(row, 4)
    place_at = jnp.where((tile == own) & (row < valid), place_at, -1)
    lands = ones(lax.rem(index((n_place, total), 0), blocks) == place_at)
    from_step = lax.rem(lax.div(index((n_slot, total), 1), blocks) - own + groups, groups)
    comes = ones(fits & (slot_group == from_step))
    place = lax.dot_general(lands, comes, (((1,), (1,)), ((), ())), preferred_element_type=F32)
    from_date = lax.rem(lax.div(index((n_place, n_slot), 1), cap), dates_dev)
    place = jnp.where(from_date == lax.div(index((n_place, n_slot), 0), blocks), place, 0.0)
    return select.astype(BF16), place.astype(BF16)


def kernel(cfg, slc_hbm, foot_hbm, valid_ref, pairs_hbm, out_ref, *scratch):
    groups, n_date, dates_dev, blocks, width, cap, slots = cfg
    out_bufs, slot_bufs = scratch[:CHUNKS], scratch[CHUNKS : 2 * CHUNKS]
    panels = scratch[2 * CHUNKS : 3 * CHUNKS]
    rest = scratch[3 * CHUNKS :]
    floor_ref, z_send, z_recv, d_send, d_recv, f_send, f_recv, c_send, c_recv = rest[:9]
    slc_ref, foot_ref, pairs_ref, in_sem = rest[9:]
    wc = width // CHUNKS
    looks = blocks // 4
    dates = n_date * dates_dev
    own, date = lax.axis_index("space"), lax.axis_index("date")
    sibling, targets, sources = partners(date, n_date)
    peers = [lax.rem(own + k, groups) for k in range(1, groups)]

    barrier = pltpu.get_barrier_semaphore()
    for peer in peers:
        pl.semaphore_signal(barrier, inc=1, device_id={"space": peer}, device_id_type=MESH)
    for target in targets + [sibling]:
        pl.semaphore_signal(barrier, inc=1, device_id={"date": target}, device_id_type=MESH)

    fetches = [
        pltpu.make_async_copy(src, dst, in_sem.at[k])
        for k, (src, dst) in enumerate([(foot_hbm, foot_ref), (slc_hbm, slc_ref), (pairs_hbm, pairs_ref)])
    ]
    for fetch in fetches:
        fetch.start()
    fetches[0].wait()
    select, place = tables(cfg, foot_ref[...], valid_ref[0], own)
    fetches[1].wait()
    fetches[2].wait()

    def gather_rows(c):
        for part in range(2):
            cols = slice(part * width + c * wc, part * width + c * wc + wc)
            half = slice(part * wc, (part + 1) * wc)
            rows = jnp.dot(select, slc_ref[:, cols], preferred_element_type=F32).astype(BF16)
            rows = rows.reshape(groups, dates_dev * cap, wc)
            slot_bufs[c][date, 0, :, half] = rows[0]
            out_bufs[c][:, :, half] = rows[1:]

    def z_copy(c, k):
        return pltpu.make_async_remote_copy(
            src_ref=out_bufs[c].at[k],
            dst_ref=slot_bufs[c].at[date, groups - 1 - k],
            send_sem=z_send.at[c, k],
            recv_sem=z_recv.at[c, k],
            device_id={"space": peers[k]},
            device_id_type=MESH,
        )

    def slot_copy(c, part, target, send_sem, recv_sem):
        steps = pl.ds(0, 1) if part == 0 else pl.ds(1, groups - 1)
        block = slot_bufs[c].at[date, steps]
        return pltpu.make_async_remote_copy(
            src_ref=block,
            dst_ref=block,
            send_sem=send_sem,
            recv_sem=recv_sem,
            device_id={"date": target},
            device_id_type=MESH,
        )

    z_copies, d_copies, s_copies, r_copies = {}, {}, {}, {}

    def send(c, part):
        for k, target in enumerate(targets):
            d_copies[c, part, k] = slot_copy(c, part, target, d_send.at[c, part, k], d_recv.at[c, part, k])
            d_copies[c, part, k].start()

    def panel_copy(c, source, send_sem, recv_sem):
        block = panels[c].at[pl.ds(source * dates_dev, dates_dev)]
        return pltpu.make_async_remote_copy(
            src_ref=block,
            dst_ref=block,
            send_sem=send_sem,
            recv_sem=recv_sem,
            device_id={"date": sibling},
            device_id_type=MESH,
        )

    def fill(c, source):
        rows = slot_bufs[c][source].reshape(groups * dates_dev * cap, 2 * wc)
        tile = jnp.dot(place, rows, preferred_element_type=F32).astype(BF16)
        panels[c][pl.ds(source * dates_dev, dates_dev)] = tile.reshape(dates_dev, blocks, 2 * wc)

    def to_sibling(c, k):
        for part in range(2):
            d_copies[c, part, k].wait_recv()
        fill(c, sources[k])
        r_copies[c, k] = panel_copy(c, sources[k], f_send.at[c, k], f_recv.at[c, k])
        r_copies[c, k].start()

    def stage_send(c):
        gather_rows(c)
        if c == 0:
            pl.semaphore_wait(barrier, len(peers) + len(targets) + 1)
        for k in range(len(peers)):
            z_copies[c, k] = z_copy(c, k)
            z_copies[c, k].start()
        send(c, 0)

    def stage_z(c):
        for k in range(len(peers)):
            z_copies[c, k].wait_recv()
        send(c, 1)

    def stage_own(c):
        fill(c, date)
        s_copies[c] = panel_copy(c, date, c_send.at[c], c_recv.at[c])
        s_copies[c].start()

    def stage_forward(c):
        for k in range(len(sources)):
            to_sibling(c, k)

    def row_sum(field):
        quads = field.reshape(4, looks, field.shape[1])
        last = lax.broadcasted_iota(jnp.int32, quads[0].shape, 0) == looks - 1
        below = jnp.where(last, 0.0, pltpu.roll(quads[0], looks - 1, 0))
        return (quads[0] + quads[1]) + (quads[2] + quads[3]) + below

    def col_sum(rows, table):
        return jnp.dot(rows.astype(BF16), table, preferred_element_type=F32)

    def stage_looks(c):
        s_copies[c].wait_recv()
        for k in range(len(sources)):
            r_copies[c, k].wait_recv()
        panel = panels[c]
        col_in = lax.broadcasted_iota(jnp.int32, (wc, 128), 0) + c * wc
        col_out = lax.broadcasted_iota(jnp.int32, (wc, 128), 1)
        table = (jnp.abs(col_in - 4 * col_out - 2) <= 5).astype(F32).astype(BF16)
        last = c == CHUNKS - 1

        group = largest_divisor(dates, max(1, GROUP_ROWS // blocks))

        def power_body(n, carry):
            sums = []
            for g in range(group):
                rows = panel[n * group + g].astype(F32)
                real, imag = rows[:, :wc], rows[:, wc:]
                sums.append(row_sum(real * real + imag * imag))
            looked = col_sum(jnp.concatenate(sums, axis=0), table).reshape(group, looks, 128)
            at = pl.ds(n * group, group)
            if c > 0:
                looked = looked + floor_ref[at]
            if last:
                looked = lax.rsqrt(jnp.maximum(looked, 1.0))
            floor_ref[at] = looked
            return carry

        lax.fori_loop(0, dates // group, power_body, 0, unroll=True)

        batch = largest_divisor(slots, max(1, BATCH_ROWS // blocks))

        def pair_body(n, carry):
            sums, scales = [], []
            for g in range(batch):
                p = n * batch + g
                i, j = pairs_ref[0, p], pairs_ref[1, p]
                first, second = panel[i].astype(F32), panel[j].astype(F32)
                ra, ia, rb, ib = first[:, :wc], first[:, wc:], second[:, :wc], second[:, wc:]
                sums.append(row_sum(ra * rb + ia * ib))
                sums.append(row_sum(ia * rb - ra * ib))
                if last:
                    scales.append(floor_ref[i] * floor_ref[j])
            looked = col_sum(jnp.concatenate(sums, axis=0), table).reshape(batch, 2, looks, 128)
            at = pl.ds(n * batch, batch)
            if c > 0:
                looked = looked + out_ref[at]
            if last:
                looked = looked * jnp.stack(scales)[:, None]
            out_ref[at] = looked
            return carry

        lax.fori_loop(0, slots // batch, pair_body, 0, unroll=True)

    for c in range(CHUNKS):
        stage_send(c)
    for c in range(CHUNKS):
        stage_z(c)
    for c in range(CHUNKS):
        stage_own(c)
    for c in range(CHUNKS):
        stage_forward(c)
        if c > 1:
            stage_looks(c - 2)
    for c in range(max(CHUNKS - 2, 0), CHUNKS):
        stage_looks(c)
    for copies in (z_copies, d_copies, s_copies, r_copies):
        for copy in copies.values():
            copy.wait_send()


def on_device(slc, footprint, valid_rows, pair_dates):
    groups, n_date = lax.axis_size("space"), lax.axis_size("date")
    dates_dev, blocks, twice = slc.shape
    width = twice // 2
    cap = blocks // groups
    slots = pair_dates.shape[0]
    looks = blocks // 4
    wc = width // CHUNKS
    others = n_date // 2 - 1
    sem = pltpu.SemaphoreType.DMA
    cfg = (groups, n_date, dates_dev, blocks, width, cap, slots)
    far = functools.partial(pltpu.with_memory_space_constraint, memory_space=pltpu.HBM)
    hbm, smem = pl.BlockSpec(memory_space=pltpu.HBM), pl.BlockSpec(memory_space=pltpu.SMEM)
    result = pl.pallas_call(
        functools.partial(kernel, cfg),
        out_shape=jax.ShapeDtypeStruct((slots, 2, looks, 128), F32),
        in_specs=[hbm, hbm, smem, hbm],
        out_specs=pl.BlockSpec(memory_space=pltpu.VMEM),
        scratch_shapes=[pltpu.VMEM((groups - 1, dates_dev * cap, 2 * wc), BF16)] * CHUNKS
        + [pltpu.VMEM((n_date, groups, dates_dev * cap, 2 * wc), BF16)] * CHUNKS
        + [pltpu.VMEM((n_date * dates_dev, blocks, 2 * wc), BF16)] * CHUNKS
        + [
            pltpu.VMEM((n_date * dates_dev, looks, 128), F32),
            sem((CHUNKS, groups - 1)),
            sem((CHUNKS, groups - 1)),
            sem((CHUNKS, 2, others)),
            sem((CHUNKS, 2, others)),
            sem((CHUNKS, others)),
            sem((CHUNKS, others)),
            sem((CHUNKS,)),
            sem((CHUNKS,)),
            pltpu.VMEM((dates_dev * blocks, twice), BF16),
            pltpu.VMEM(footprint.shape[::-1], jnp.int32),
            pltpu.SMEM(pair_dates.shape[::-1], jnp.int32),
            sem((3,)),
        ],
        compiler_params=pltpu.CompilerParams(
            collective_id=0, has_side_effects=True, vmem_limit_bytes=40 * 1024 * 1024
        ),
    )(far(slc.reshape(dates_dev * blocks, twice)), far(footprint.T), valid_rows, far(pair_dates.T))
    return result[:, None]


def solution(mesh):
    in_specs = (P("date", "space", None), P(), P("space"), P("date", None))
    out_specs = P("date", "space", None, None, None)
    return jax.shard_map(
        on_device, mesh=mesh, in_specs=in_specs, out_specs=out_specs, check_vma=False
    )
```

```python
import functools

import jax
import jax.numpy as jnp
from jax import lax
from jax.experimental import pallas as pl
from jax.experimental.pallas import tpu as pltpu
from jax.sharding import PartitionSpec as P

CHUNKS = 4
BATCH_ROWS, GROUP_ROWS = 1056, 1024
MESH = pl.DeviceIdType.MESH
F32, BF16 = jnp.float32, jnp.bfloat16


def largest_divisor(count, most):
    return max(g for g in range(1, most + 1) if count % g == 0)


def partners(date, n_date):
    chips = n_date // 2
    chip, core = date // 2, date % 2
    sibling = chip * 2 + (1 - core)
    targets = [lax.rem(chip + k, chips) * 2 + core for k in range(1, chips)]
    sources = [lax.rem(chip + chips - k, chips) * 2 + core for k in range(1, chips)]
    return sibling, targets, sources


def tables(cfg, foot, valid, own):
    groups, n_date, dates_dev, blocks, width, cap, slots = cfg
    total, looks, lane = groups * blocks, blocks // 4, 128
    tile, row = foot[0:1], foot[1:2]
    tile_step = jnp.where(tile < 0, -1, lax.rem(tile - own + groups, groups))

    def index(shape, dim):
        return lax.broadcasted_iota(jnp.int32, shape, dim)

    def ones(mask):
        return mask.astype(F32).astype(BF16)

    earlier = (index((lane, lane), 0) < index((lane, lane), 1)) & (
        lax.div(index((lane, lane), 0), blocks) == lax.div(index((lane, lane), 1), blocks)
    )
    ranks = []
    for at in range(0, total, lane):
        hot = index((max(groups, 8), lane), 0) == tile[:, at : at + lane]
        count = jnp.dot(ones(hot), ones(earlier), preferred_element_type=F32)
        ranks.append(jnp.sum(jnp.where(hot, count, 0.0), axis=0, keepdims=True))
    rank = jnp.concatenate(ranks, axis=1).astype(jnp.int32)

    n_slot, n_place = groups * dates_dev * cap, dates_dev * blocks
    slot = index((n_slot, total), 0)
    slot_group, slot_rank = lax.div(slot, dates_dev * cap), lax.rem(slot, cap)
    slot_date = lax.rem(lax.div(index((n_slot, n_place), 0), cap), dates_dev)
    fits = slot_rank == rank
    leaves = ones(fits & (slot_group == tile_step))
    held = ones(index((total, n_place), 0) == own * blocks + lax.rem(index((total, n_place), 1), blocks))
    select = jnp.dot(leaves, held, preferred_element_type=F32)
    select = jnp.where(slot_date == lax.div(index((n_slot, n_place), 1), blocks), select, 0.0)

    place_at = lax.rem(row, 4) * looks + lax.div(row, 4)
    place_at = jnp.where((tile == own) & (row < valid), place_at, -1)
    lands = ones(lax.rem(index((n_place, total), 0), blocks) == place_at)
    from_step = lax.rem(lax.div(index((n_slot, total), 1), blocks) - own + groups, groups)
    comes = ones(fits & (slot_group == from_step))
    place = lax.dot_general(lands, comes, (((1,), (1,)), ((), ())), preferred_element_type=F32)
    from_date = lax.rem(lax.div(index((n_place, n_slot), 1), cap), dates_dev)
    place = jnp.where(from_date == lax.div(index((n_place, n_slot), 0), blocks), place, 0.0)
    return select.astype(BF16), place.astype(BF16)


def kernel(cfg, slc_hbm, foot_hbm, valid_ref, pairs_hbm, out_ref, *scratch):
    groups, n_date, dates_dev, blocks, width, cap, slots = cfg
    out_bufs, slot_bufs = scratch[:CHUNKS], scratch[CHUNKS : 2 * CHUNKS]
    panels = scratch[2 * CHUNKS : 3 * CHUNKS]
    rest = scratch[3 * CHUNKS :]
    floor_ref, z_send, z_recv, d_send, d_recv, f_send, f_recv, c_send, c_recv = rest[:9]
    slc_ref, foot_ref, pairs_ref, in_sem = rest[9:]
    wc = width // CHUNKS
    looks = blocks // 4
    dates = n_date * dates_dev
    own, date = lax.axis_index("space"), lax.axis_index("date")
    sibling, targets, sources = partners(date, n_date)
    peers = [lax.rem(own + k, groups) for k in range(1, groups)]

    barrier = pltpu.get_barrier_semaphore()
    for peer in peers:
        pl.semaphore_signal(barrier, inc=1, device_id={"space": peer}, device_id_type=MESH)
    for target in targets + [sibling]:
        pl.semaphore_signal(barrier, inc=1, device_id={"date": target}, device_id_type=MESH)

    fetches = [
        pltpu.make_async_copy(src, dst, in_sem.at[k])
        for k, (src, dst) in enumerate([(foot_hbm, foot_ref), (slc_hbm, slc_ref), (pairs_hbm, pairs_ref)])
    ]
    for fetch in fetches:
        fetch.start()
    fetches[0].wait()
    select, place = tables(cfg, foot_ref[...], valid_ref[0], own)
    fetches[1].wait()

    def gather_rows(c):
        for part in range(2):
            cols = slice(part * width + c * wc, part * width + c * wc + wc)
            half = slice(part * wc, (part + 1) * wc)
            rows = jnp.dot(select, slc_ref[:, cols], preferred_element_type=F32).astype(BF16)
            rows = rows.reshape(groups, dates_dev * cap, wc)
            slot_bufs[c][date, 0, :, half] = rows[0]
            out_bufs[c][:, :, half] = rows[1:]

    def z_copy(c, k):
        return pltpu.make_async_remote_copy(
            src_ref=out_bufs[c].at[k],
            dst_ref=slot_bufs[c].at[date, groups - 1 - k],
            send_sem=z_send.at[c, k],
            recv_sem=z_recv.at[c, k],
            device_id={"space": peers[k]},
            device_id_type=MESH,
        )

    def slot_copy(c, part, target, send_sem, recv_sem):
        steps = pl.ds(0, 1) if part == 0 else pl.ds(1, groups - 1)
        block = slot_bufs[c].at[date, steps]
        return pltpu.make_async_remote_copy(
            src_ref=block,
            dst_ref=block,
            send_sem=send_sem,
            recv_sem=recv_sem,
            device_id={"date": target},
            device_id_type=MESH,
        )

    z_copies, d_copies, s_copies, r_copies = {}, {}, {}, {}

    def send(c, part):
        for k, target in enumerate(targets):
            d_copies[c, part, k] = slot_copy(c, part, target, d_send.at[c, part, k], d_recv.at[c, part, k])
            d_copies[c, part, k].start()

    def panel_copy(c, source, send_sem, recv_sem):
        block = panels[c].at[pl.ds(source * dates_dev, dates_dev)]
        return pltpu.make_async_remote_copy(
            src_ref=block,
            dst_ref=block,
            send_sem=send_sem,
            recv_sem=recv_sem,
            device_id={"date": sibling},
            device_id_type=MESH,
        )

    def fill(c, source):
        rows = slot_bufs[c][source].reshape(groups * dates_dev * cap, 2 * wc)
        tile = jnp.dot(place, rows, preferred_element_type=F32).astype(BF16)
        panels[c][pl.ds(source * dates_dev, dates_dev)] = tile.reshape(dates_dev, blocks, 2 * wc)

    def stage_send(c):
        gather_rows(c)
        if c == 0:
            pl.semaphore_wait(barrier, len(peers) + len(targets) + 1)
        for k in range(len(peers)):
            z_copies[c, k] = z_copy(c, k)
            z_copies[c, k].start()
        send(c, 0)

    def stage_z(c):
        for k in range(len(peers)):
            z_copies[c, k].wait_recv()
        send(c, 1)

    def stage_own(c):
        fill(c, date)
        s_copies[c] = panel_copy(c, date, c_send.at[c], c_recv.at[c])
        s_copies[c].start()

    def stage_forward(c):
        for k in range(len(sources)):
            for part in range(2):
                d_copies[c, part, k].wait_recv()
        for k in range(len(sources)):
            fill(c, sources[k])
        for k in range(len(sources)):
            r_copies[c, k] = panel_copy(c, sources[k], f_send.at[c, k], f_recv.at[c, k])
            r_copies[c, k].start()

    def row_sum(field):
        quads = field.reshape(4, looks, field.shape[1])
        last = lax.broadcasted_iota(jnp.int32, quads[0].shape, 0) == looks - 1
        below = jnp.where(last, 0.0, pltpu.roll(quads[0], looks - 1, 0))
        return (quads[0] + quads[1]) + (quads[2] + quads[3]) + below

    def col_sum(rows, table):
        return jnp.dot(rows.astype(BF16), table, preferred_element_type=F32)

    def stage_looks(c):
        s_copies[c].wait_recv()
        for k in range(len(sources)):
            r_copies[c, k].wait_recv()
        panel = panels[c]
        col_in = lax.broadcasted_iota(jnp.int32, (wc, 128), 0) + c * wc
        col_out = lax.broadcasted_iota(jnp.int32, (wc, 128), 1)
        table = (jnp.abs(col_in - 4 * col_out - 2) <= 5).astype(F32).astype(BF16)
        last = c == CHUNKS - 1

        group = largest_divisor(dates, max(1, GROUP_ROWS // blocks))

        def power_body(n, carry):
            sums = []
            for g in range(group):
                rows = panel[n * group + g].astype(F32)
                real, imag = rows[:, :wc], rows[:, wc:]
                sums.append(row_sum(real * real + imag * imag))
            looked = col_sum(jnp.concatenate(sums, axis=0), table).reshape(group, looks, 128)
            at = pl.ds(n * group, group)
            if c > 0:
                looked = looked + floor_ref[at]
            if last:
                looked = lax.rsqrt(jnp.maximum(looked, 1.0))
            floor_ref[at] = looked
            return carry

        lax.fori_loop(0, dates // group, power_body, 0, unroll=True)

        batch = largest_divisor(slots, max(1, BATCH_ROWS // blocks))

        def pair_body(n, carry):
            sums, scales = [], []
            for g in range(batch):
                p = n * batch + g
                i, j = pairs_ref[0, p], pairs_ref[1, p]
                first, second = panel[i].astype(F32), panel[j].astype(F32)
                ra, ia, rb, ib = first[:, :wc], first[:, wc:], second[:, :wc], second[:, wc:]
                sums.append(row_sum(ra * rb + ia * ib))
                sums.append(row_sum(ia * rb - ra * ib))
                if last:
                    scales.append(floor_ref[i] * floor_ref[j])
            looked = col_sum(jnp.concatenate(sums, axis=0), table).reshape(batch, 2, looks, 128)
            at = pl.ds(n * batch, batch)
            if c > 0:
                looked = looked + out_ref[at]
            if last:
                looked = looked * jnp.stack(scales)[:, None]
            out_ref[at] = looked
            return carry

        lax.fori_loop(0, slots // batch, pair_body, 0, unroll=True)

    for c in range(CHUNKS):
        stage_send(c)
    for c in range(CHUNKS):
        stage_z(c)
    for c in range(CHUNKS):
        stage_own(c)
    fetches[2].wait()
    for c in range(CHUNKS):
        stage_forward(c)
        if c > 1:
            stage_looks(c - 2)
    for c in range(max(CHUNKS - 2, 0), CHUNKS):
        stage_looks(c)
    for copies in (z_copies, d_copies, s_copies, r_copies):
        for copy in copies.values():
            copy.wait_send()


def on_device(slc, footprint, valid_rows, pair_dates):
    groups, n_date = lax.axis_size("space"), lax.axis_size("date")
    dates_dev, blocks, twice = slc.shape
    width = twice // 2
    cap = blocks // groups
    slots = pair_dates.shape[0]
    looks = blocks // 4
    wc = width // CHUNKS
    others = n_date // 2 - 1
    sem = pltpu.SemaphoreType.DMA
    cfg = (groups, n_date, dates_dev, blocks, width, cap, slots)
    far = functools.partial(pltpu.with_memory_space_constraint, memory_space=pltpu.HBM)
    hbm, smem = pl.BlockSpec(memory_space=pltpu.HBM), pl.BlockSpec(memory_space=pltpu.SMEM)
    result = pl.pallas_call(
        functools.partial(kernel, cfg),
        out_shape=jax.ShapeDtypeStruct((slots, 2, looks, 128), F32),
        in_specs=[hbm, hbm, smem, hbm],
        out_specs=pl.BlockSpec(memory_space=pltpu.VMEM),
        scratch_shapes=[pltpu.VMEM((groups - 1, dates_dev * cap, 2 * wc), BF16)] * CHUNKS
        + [pltpu.VMEM((n_date, groups, dates_dev * cap, 2 * wc), BF16)] * CHUNKS
        + [pltpu.VMEM((n_date * dates_dev, blocks, 2 * wc), BF16)] * CHUNKS
        + [
            pltpu.VMEM((n_date * dates_dev, looks, 128), F32),
            sem((CHUNKS, groups - 1)),
            sem((CHUNKS, groups - 1)),
            sem((CHUNKS, 2, others)),
            sem((CHUNKS, 2, others)),
            sem((CHUNKS, others)),
            sem((CHUNKS, others)),
            sem((CHUNKS,)),
            sem((CHUNKS,)),
            pltpu.VMEM((dates_dev * blocks, twice), BF16),
            pltpu.VMEM(footprint.shape[::-1], jnp.int32),
            pltpu.SMEM(pair_dates.shape[::-1], jnp.int32),
            sem((3,)),
        ],
        compiler_params=pltpu.CompilerParams(
            collective_id=0, has_side_effects=True, vmem_limit_bytes=40 * 1024 * 1024
        ),
    )(far(slc.reshape(dates_dev * blocks, twice)), far(footprint.T), valid_rows, far(pair_dates.T))
    return result[:, None]


def solution(mesh):
    in_specs = (P("date", "space", None), P(), P("space"), P("date", None))
    out_specs = P("date", "space", None, None, None)
    return jax.shard_map(
        on_device, mesh=mesh, in_specs=in_specs, out_specs=out_specs, check_vma=False
    )
```

```python
import functools

import jax
import jax.numpy as jnp
from jax import lax
from jax.experimental import pallas as pl
from jax.experimental.pallas import tpu as pltpu
from jax.sharding import PartitionSpec as P

CHUNKS = 4
BATCH_ROWS, GROUP_ROWS = 1056, 1024
MESH = pl.DeviceIdType.MESH
F32, BF16 = jnp.float32, jnp.bfloat16


def largest_divisor(count, most):
    return max(g for g in range(1, most + 1) if count % g == 0)


def partners(date, n_date):
    chips = n_date // 2
    chip, core = date // 2, date % 2
    sibling = chip * 2 + (1 - core)
    targets = [lax.rem(chip + k, chips) * 2 + core for k in range(1, chips)]
    sources = [lax.rem(chip + chips - k, chips) * 2 + core for k in range(1, chips)]
    return sibling, targets, sources


def tables(cfg, foot, valid, own):
    groups, n_date, dates_dev, blocks, width, cap, slots = cfg
    total, looks, lane = groups * blocks, blocks // 4, 128
    tile, row = foot[0:1], foot[1:2]
    tile_step = jnp.where(tile < 0, -1, lax.rem(tile - own + groups, groups))

    def index(shape, dim):
        return lax.broadcasted_iota(jnp.int32, shape, dim)

    def ones(mask):
        return mask.astype(F32).astype(BF16)

    earlier = (index((lane, lane), 0) < index((lane, lane), 1)) & (
        lax.div(index((lane, lane), 0), blocks) == lax.div(index((lane, lane), 1), blocks)
    )
    ranks = []
    for at in range(0, total, lane):
        hot = index((max(groups, 8), lane), 0) == tile[:, at : at + lane]
        count = jnp.dot(ones(hot), ones(earlier), preferred_element_type=F32)
        ranks.append(jnp.sum(jnp.where(hot, count, 0.0), axis=0, keepdims=True))
    rank = jnp.concatenate(ranks, axis=1).astype(jnp.int32)

    n_slot, n_place = groups * dates_dev * cap, dates_dev * blocks
    slot = index((n_slot, total), 0)
    slot_group, slot_rank = lax.div(slot, dates_dev * cap), lax.rem(slot, cap)
    slot_date = lax.rem(lax.div(index((n_slot, n_place), 0), cap), dates_dev)
    fits = slot_rank == rank
    leaves = ones(fits & (slot_group == tile_step))
    held = ones(index((total, n_place), 0) == own * blocks + lax.rem(index((total, n_place), 1), blocks))
    select = jnp.dot(leaves, held, preferred_element_type=F32)
    select = jnp.where(slot_date == lax.div(index((n_slot, n_place), 1), blocks), select, 0.0)

    place_at = lax.rem(row, 4) * looks + lax.div(row, 4)
    place_at = jnp.where((tile == own) & (row < valid), place_at, -1)
    lands = ones(lax.rem(index((n_place, total), 0), blocks) == place_at)
    from_step = lax.rem(lax.div(index((n_slot, total), 1), blocks) - own + groups, groups)
    comes = ones(fits & (slot_group == from_step))
    place = lax.dot_general(lands, comes, (((1,), (1,)), ((), ())), preferred_element_type=F32)
    from_date = lax.rem(lax.div(index((n_place, n_slot), 1), cap), dates_dev)
    place = jnp.where(from_date == lax.div(index((n_place, n_slot), 0), blocks), place, 0.0)
    return select.astype(BF16), place.astype(BF16)


def kernel(cfg, slc_hbm, foot_hbm, valid_ref, pairs_hbm, out_ref, *scratch):
    groups, n_date, dates_dev, blocks, width, cap, slots = cfg
    out_bufs, slot_bufs = scratch[:CHUNKS], scratch[CHUNKS : 2 * CHUNKS]
    panels = scratch[2 * CHUNKS : 3 * CHUNKS]
    rest = scratch[3 * CHUNKS :]
    floor_ref, z_send, z_recv, d_send, d_recv, f_send, f_recv, c_send, c_recv = rest[:9]
    slc_ref, foot_ref, pairs_ref, in_sem = rest[9:]
    wc = width // CHUNKS
    looks = blocks // 4
    dates = n_date * dates_dev
    own, date = lax.axis_index("space"), lax.axis_index("date")
    sibling, targets, sources = partners(date, n_date)
    peers = [lax.rem(own + k, groups) for k in range(1, groups)]

    barrier = pltpu.get_barrier_semaphore()
    for peer in peers:
        pl.semaphore_signal(barrier, inc=1, device_id={"space": peer}, device_id_type=MESH)
    for target in targets + [sibling]:
        pl.semaphore_signal(barrier, inc=1, device_id={"date": target}, device_id_type=MESH)

    fetches = [
        pltpu.make_async_copy(src, dst, in_sem.at[k])
        for k, (src, dst) in enumerate([(foot_hbm, foot_ref), (slc_hbm, slc_ref), (pairs_hbm, pairs_ref)])
    ]
    for fetch in fetches:
        fetch.start()
    fetches[0].wait()
    select, place = tables(cfg, foot_ref[...], valid_ref[0], own)
    fetches[1].wait()

    def gather_rows(c):
        for part in range(2):
            cols = slice(part * width + c * wc, part * width + c * wc + wc)
            half = slice(part * wc, (part + 1) * wc)
            rows = jnp.dot(select, slc_ref[:, cols], preferred_element_type=F32).astype(BF16)
            rows = rows.reshape(groups, dates_dev * cap, wc)
            slot_bufs[c][date, 0, :, half] = rows[0]
            out_bufs[c][:, :, half] = rows[1:]

    def z_copy(c, k):
        return pltpu.make_async_remote_copy(
            src_ref=out_bufs[c].at[k],
            dst_ref=slot_bufs[c].at[date, groups - 1 - k],
            send_sem=z_send.at[c, k],
            recv_sem=z_recv.at[c, k],
            device_id={"space": peers[k]},
            device_id_type=MESH,
        )

    def slot_copy(c, part, target, send_sem, recv_sem):
        steps = pl.ds(0, 1) if part == 0 else pl.ds(1, groups - 1)
        block = slot_bufs[c].at[date, steps]
        return pltpu.make_async_remote_copy(
            src_ref=block,
            dst_ref=block,
            send_sem=send_sem,
            recv_sem=recv_sem,
            device_id={"date": target},
            device_id_type=MESH,
        )

    z_copies, d_copies, s_copies, r_copies = {}, {}, {}, {}

    def send(c, part):
        for k, target in enumerate(targets):
            d_copies[c, part, k] = slot_copy(c, part, target, d_send.at[c, part, k], d_recv.at[c, part, k])
            d_copies[c, part, k].start()

    def panel_copy(c, source, send_sem, recv_sem):
        block = panels[c].at[pl.ds(source * dates_dev, dates_dev)]
        return pltpu.make_async_remote_copy(
            src_ref=block,
            dst_ref=block,
            send_sem=send_sem,
            recv_sem=recv_sem,
            device_id={"date": sibling},
            device_id_type=MESH,
        )

    def fill(c, source):
        rows = slot_bufs[c][source].reshape(groups * dates_dev * cap, 2 * wc)
        tile = jnp.dot(place, rows, preferred_element_type=F32).astype(BF16)
        panels[c][pl.ds(source * dates_dev, dates_dev)] = tile.reshape(dates_dev, blocks, 2 * wc)

    def stage_send(c):
        gather_rows(c)
        if c == 0:
            pl.semaphore_wait(barrier, len(peers) + len(targets) + 1)
        for k in range(len(peers)):
            z_copies[c, k] = z_copy(c, k)
            z_copies[c, k].start()
        send(c, 0)

    def stage_z(c):
        for k in range(len(peers)):
            z_copies[c, k].wait_recv()
        send(c, 1)

    def stage_own(c):
        fill(c, date)
        s_copies[c] = panel_copy(c, date, c_send.at[c], c_recv.at[c])
        s_copies[c].start()

    def stage_forward(c):
        for k in range(len(sources)):
            for part in range(2):
                d_copies[c, part, k].wait_recv()
        for k in range(len(sources)):
            fill(c, sources[k])
        for k in range(len(sources)):
            r_copies[c, k] = panel_copy(c, sources[k], f_send.at[c, k], f_recv.at[c, k])
            r_copies[c, k].start()

    def row_sum(field):
        quads = field.reshape(4, looks, field.shape[1])
        last = lax.broadcasted_iota(jnp.int32, quads[0].shape, 0) == looks - 1
        below = jnp.where(last, 0.0, pltpu.roll(quads[0], looks - 1, 0))
        return (quads[0] + quads[1]) + (quads[2] + quads[3]) + below

    def col_sum(rows, table):
        return jnp.dot(rows.astype(BF16), table, preferred_element_type=F32)

    def stage_looks(c):
        s_copies[c].wait_recv()
        for k in range(len(sources)):
            r_copies[c, k].wait_recv()
        panel = panels[c]
        col_in = lax.broadcasted_iota(jnp.int32, (wc, 128), 0) + c * wc
        col_out = lax.broadcasted_iota(jnp.int32, (wc, 128), 1)
        table = (jnp.abs(col_in - 4 * col_out - 2) <= 5).astype(F32).astype(BF16)
        last = c == CHUNKS - 1

        group = largest_divisor(dates, max(1, GROUP_ROWS // blocks))

        def power_body(n, carry):
            sums = []
            for g in range(group):
                rows = panel[n * group + g].astype(F32)
                real, imag = rows[:, :wc], rows[:, wc:]
                sums.append(row_sum(real * real + imag * imag))
            looked = col_sum(jnp.concatenate(sums, axis=0), table).reshape(group, looks, 128)
            at = pl.ds(n * group, group)
            if c > 0:
                looked = looked + floor_ref[at]
            if last:
                looked = lax.rsqrt(jnp.maximum(looked, 1.0))
            floor_ref[at] = looked
            return carry

        lax.fori_loop(0, dates // group, power_body, 0, unroll=True)

        batch = largest_divisor(slots, max(1, BATCH_ROWS // blocks))

        def pair_body(n, carry):
            sums, scales = [], []
            for g in range(batch):
                p = n * batch + g
                i, j = pairs_ref[0, p], pairs_ref[1, p]
                first, second = panel[i].astype(F32), panel[j].astype(F32)
                ra, ia, rb, ib = first[:, :wc], first[:, wc:], second[:, :wc], second[:, wc:]
                sums.append(row_sum(ra * rb + ia * ib))
                sums.append(row_sum(ia * rb - ra * ib))
                if last:
                    scales.append(floor_ref[i] * floor_ref[j])
            looked = col_sum(jnp.concatenate(sums, axis=0), table).reshape(batch, 2, looks, 128)
            at = pl.ds(n * batch, batch)
            if c > 0:
                looked = looked + out_ref[at]
            if last:
                looked = looked * jnp.stack(scales)[:, None]
            out_ref[at] = looked
            return carry

        lax.fori_loop(0, slots // batch, pair_body, 0, unroll=True)

    for c in range(CHUNKS):
        stage_send(c)
    for c in range(CHUNKS):
        stage_z(c)
    for c in range(CHUNKS):
        stage_own(c)
    fetches[2].wait()
    for c in range(CHUNKS):
        stage_forward(c)
        if c > 0:
            stage_looks(c - 1)
    stage_looks(CHUNKS - 1)
    for copies in (z_copies, d_copies, s_copies, r_copies):
        for copy in copies.values():
            copy.wait_send()


def on_device(slc, footprint, valid_rows, pair_dates):
    groups, n_date = lax.axis_size("space"), lax.axis_size("date")
    dates_dev, blocks, twice = slc.shape
    width = twice // 2
    cap = blocks // groups
    slots = pair_dates.shape[0]
    looks = blocks // 4
    wc = width // CHUNKS
    others = n_date // 2 - 1
    sem = pltpu.SemaphoreType.DMA
    cfg = (groups, n_date, dates_dev, blocks, width, cap, slots)
    far = functools.partial(pltpu.with_memory_space_constraint, memory_space=pltpu.HBM)
    hbm, smem = pl.BlockSpec(memory_space=pltpu.HBM), pl.BlockSpec(memory_space=pltpu.SMEM)
    result = pl.pallas_call(
        functools.partial(kernel, cfg),
        out_shape=jax.ShapeDtypeStruct((slots, 2, looks, 128), F32),
        in_specs=[hbm, hbm, smem, hbm],
        out_specs=pl.BlockSpec(memory_space=pltpu.VMEM),
        scratch_shapes=[pltpu.VMEM((groups - 1, dates_dev * cap, 2 * wc), BF16)] * CHUNKS
        + [pltpu.VMEM((n_date, groups, dates_dev * cap, 2 * wc), BF16)] * CHUNKS
        + [pltpu.VMEM((n_date * dates_dev, blocks, 2 * wc), BF16)] * CHUNKS
        + [
            pltpu.VMEM((n_date * dates_dev, looks, 128), F32),
            sem((CHUNKS, groups - 1)),
            sem((CHUNKS, groups - 1)),
            sem((CHUNKS, 2, others)),
            sem((CHUNKS, 2, others)),
            sem((CHUNKS, others)),
            sem((CHUNKS, others)),
            sem((CHUNKS,)),
            sem((CHUNKS,)),
            pltpu.VMEM((dates_dev * blocks, twice), BF16),
            pltpu.VMEM(footprint.shape[::-1], jnp.int32),
            pltpu.SMEM(pair_dates.shape[::-1], jnp.int32),
            sem((3,)),
        ],
        compiler_params=pltpu.CompilerParams(
            collective_id=0, has_side_effects=True, vmem_limit_bytes=40 * 1024 * 1024
        ),
    )(far(slc.reshape(dates_dev * blocks, twice)), far(footprint.T), valid_rows, far(pair_dates.T))
    return result[:, None]


def solution(mesh):
    in_specs = (P("date", "space", None), P(), P("space"), P("date", None))
    out_specs = P("date", "space", None, None, None)
    return jax.shard_map(
        on_device, mesh=mesh, in_specs=in_specs, out_specs=out_specs, check_vma=False
    )
```

```python
import functools

import jax
import jax.numpy as jnp
from jax import lax
from jax.experimental import pallas as pl
from jax.experimental.pallas import tpu as pltpu
from jax.sharding import PartitionSpec as P

CHUNKS = 4
BATCH_ROWS = 1056
MESH = pl.DeviceIdType.MESH
F32, BF16 = jnp.float32, jnp.bfloat16


def largest_divisor(count, most):
    return max(g for g in range(1, most + 1) if count % g == 0)


def partners(date, n_date):
    chips = n_date // 2
    chip, core = date // 2, date % 2
    sibling = chip * 2 + (1 - core)
    if chips == 4:
        x, y = chip % 2, chip // 2
        near = [y * 2 + 1 - x, (1 - y) * 2 + x, (1 - y) * 2 + 1 - x]
        others = [near[k] * 2 + core for k in (2, 0, 1)]
        return sibling, others, others
    targets = [lax.rem(chip + k, chips) * 2 + core for k in range(1, chips)]
    sources = [lax.rem(chip + chips - k, chips) * 2 + core for k in range(1, chips)]
    return sibling, targets, sources


def tables(cfg, foot, valid, own):
    groups, n_date, dates_dev, blocks, width, cap, slots = cfg
    total, looks, lane = groups * blocks, blocks // 4, 128
    tile, row = foot[0:1], foot[1:2]
    tile_step = jnp.where(tile < 0, -1, lax.rem(tile - own + groups, groups))

    def index(shape, dim):
        return lax.broadcasted_iota(jnp.int32, shape, dim)

    def ones(mask):
        return mask.astype(F32).astype(BF16)

    earlier = (index((lane, lane), 0) < index((lane, lane), 1)) & (
        lax.div(index((lane, lane), 0), blocks) == lax.div(index((lane, lane), 1), blocks)
    )
    ranks = []
    for at in range(0, total, lane):
        hot = index((max(groups, 8), lane), 0) == tile[:, at : at + lane]
        count = jnp.dot(ones(hot), ones(earlier), preferred_element_type=F32)
        ranks.append(jnp.sum(jnp.where(hot, count, 0.0), axis=0, keepdims=True))
    rank = jnp.concatenate(ranks, axis=1).astype(jnp.int32)

    n_slot, n_place = groups * dates_dev * cap, dates_dev * blocks
    slot = index((n_slot, total), 0)
    slot_group, slot_rank = lax.div(slot, dates_dev * cap), lax.rem(slot, cap)
    slot_date = lax.rem(lax.div(index((n_slot, n_place), 0), cap), dates_dev)
    fits = slot_rank == rank
    leaves = ones(fits & (slot_group == tile_step))
    held = ones(index((total, n_place), 0) == own * blocks + lax.rem(index((total, n_place), 1), blocks))
    select = jnp.dot(leaves, held, preferred_element_type=F32)
    select = jnp.where(slot_date == lax.div(index((n_slot, n_place), 1), blocks), select, 0.0)

    place_at = lax.rem(row, 4) * looks + lax.div(row, 4)
    place_at = jnp.where((tile == own) & (row < valid), place_at, -1)
    lands = ones(lax.rem(index((n_place, total), 0), blocks) == place_at)
    from_step = lax.rem(lax.div(index((n_slot, total), 1), blocks) - own + groups, groups)
    comes = ones(fits & (slot_group == from_step))
    place = lax.dot_general(lands, comes, (((1,), (1,)), ((), ())), preferred_element_type=F32)
    from_date = lax.rem(lax.div(index((n_place, n_slot), 1), cap), dates_dev)
    place = jnp.where(from_date == lax.div(index((n_place, n_slot), 0), blocks), place, 0.0)
    return select.astype(BF16), place.astype(BF16)


def kernel(cfg, slc_hbm, foot_hbm, valid_ref, pairs_hbm, out_ref, *scratch):
    groups, n_date, dates_dev, blocks, width, cap, slots = cfg
    out_bufs, slot_bufs = scratch[:CHUNKS], scratch[CHUNKS : 2 * CHUNKS]
    panels = scratch[2 * CHUNKS : 3 * CHUNKS]
    rest = scratch[3 * CHUNKS :]
    floor_ref, z_send, z_recv, d_send, d_recv, f_send, f_recv, c_send, c_recv = rest[:9]
    slc_ref, foot_ref, pairs_ref, in_sem = rest[9:]
    wc = width // CHUNKS
    looks = blocks // 4
    dates = n_date * dates_dev
    own, date = lax.axis_index("space"), lax.axis_index("date")
    sibling, targets, sources = partners(date, n_date)
    across = partners(sibling, n_date)[2]
    peers = [lax.rem(own + k, groups) for k in range(1, groups)]

    barrier = pltpu.get_barrier_semaphore()
    for peer in peers:
        pl.semaphore_signal(barrier, inc=1, device_id={"space": peer}, device_id_type=MESH)
    for target in targets + [sibling]:
        pl.semaphore_signal(barrier, inc=1, device_id={"date": target}, device_id_type=MESH)

    fetches = [
        pltpu.make_async_copy(src, dst, in_sem.at[k])
        for k, (src, dst) in enumerate([(foot_hbm, foot_ref), (slc_hbm, slc_ref), (pairs_hbm, pairs_ref)])
    ]
    for fetch in fetches:
        fetch.start()
    fetches[0].wait()
    select, place = tables(cfg, foot_ref[...], valid_ref[0], own)
    fetches[1].wait()

    def gather_rows(c):
        for part in range(2):
            cols = slice(part * width + c * wc, part * width + c * wc + wc)
            half = slice(part * wc, (part + 1) * wc)
            rows = jnp.dot(select, slc_ref[:, cols], preferred_element_type=F32).astype(BF16)
            rows = rows.reshape(groups, dates_dev * cap, wc)
            slot_bufs[c][date, 0, :, half] = rows[0]
            out_bufs[c][:, :, half] = rows[1:]

    def z_copy(c, k):
        return pltpu.make_async_remote_copy(
            src_ref=out_bufs[c].at[k],
            dst_ref=slot_bufs[c].at[date, groups - 1 - k],
            send_sem=z_send.at[c, k],
            recv_sem=z_recv.at[c, k],
            device_id={"space": peers[k]},
            device_id_type=MESH,
        )

    def slot_copy(c, part, target, send_sem, recv_sem):
        steps = pl.ds(0, 1) if part == 0 else pl.ds(1, groups - 1)
        block = slot_bufs[c].at[date, steps]
        return pltpu.make_async_remote_copy(
            src_ref=block,
            dst_ref=block,
            send_sem=send_sem,
            recv_sem=recv_sem,
            device_id={"date": target},
            device_id_type=MESH,
        )

    z_copies, d_copies, s_copies, r_copies = {}, {}, {}, {}

    def send(c, part):
        for k, target in enumerate(targets):
            d_copies[c, part, k] = slot_copy(c, part, target, d_send.at[c, part, k], d_recv.at[c, part, k])
            d_copies[c, part, k].start()

    def panel_copy(c, source, send_sem, recv_sem):
        block = panels[c].at[pl.ds(source * dates_dev, dates_dev)]
        return pltpu.make_async_remote_copy(
            src_ref=block,
            dst_ref=block,
            send_sem=send_sem,
            recv_sem=recv_sem,
            device_id={"date": sibling},
            device_id_type=MESH,
        )

    def fill(c, source):
        rows = slot_bufs[c][source].reshape(groups * dates_dev * cap, 2 * wc)
        tile = jnp.dot(place, rows, preferred_element_type=F32).astype(BF16)
        panels[c][pl.ds(source * dates_dev, dates_dev)] = tile.reshape(dates_dev, blocks, 2 * wc)

    def stage_send(c):
        gather_rows(c)
        if c == 0:
            pl.semaphore_wait(barrier, len(peers) + len(targets) + 1)
        for k in range(len(peers)):
            z_copies[c, k] = z_copy(c, k)
            z_copies[c, k].start()
        send(c, 0)

    def stage_z(c):
        for k in range(len(peers)):
            z_copies[c, k].wait_recv()
        send(c, 1)

    def stage_own(c):
        fill(c, date)
        s_copies[c] = panel_copy(c, date, c_send.at[c], c_recv.at[c])
        s_copies[c].start()

    def stage_forward(c):
        for k in range(len(sources)):
            for part in range(2):
                d_copies[c, part, k].wait_recv()
        for k in range(len(sources)):
            fill(c, sources[k])
        for k in range(len(sources)):
            r_copies[c, k] = panel_copy(c, sources[k], f_send.at[c, k], f_recv.at[c, k])
            r_copies[c, k].start()

    def row_sum(field):
        quads = field.reshape(4, looks, field.shape[1])
        last = lax.broadcasted_iota(jnp.int32, quads[0].shape, 0) == looks - 1
        below = jnp.where(last, 0.0, pltpu.roll(quads[0], looks - 1, 0))
        return (quads[0] + quads[1]) + (quads[2] + quads[3]) + below

    def col_sum(rows, table):
        return jnp.dot(rows.astype(BF16), table, preferred_element_type=F32)

    def stage_looks(c):
        panel = panels[c]
        col_in = lax.broadcasted_iota(jnp.int32, (wc, 128), 0) + c * wc
        col_out = lax.broadcasted_iota(jnp.int32, (wc, 128), 1)
        table = (jnp.abs(col_in - 4 * col_out - 2) <= 5).astype(F32).astype(BF16)
        last = c == CHUNKS - 1

        def powers(blocks_of):
            sums = []
            for source in blocks_of:
                for d in range(dates_dev):
                    rows = panel[source * dates_dev + d].astype(F32)
                    real, imag = rows[:, :wc], rows[:, wc:]
                    sums.append(row_sum(real * real + imag * imag))
            looked = col_sum(jnp.concatenate(sums, axis=0), table)
            looked = looked.reshape(len(blocks_of), dates_dev, looks, 128)
            for n, source in enumerate(blocks_of):
                at = pl.ds(source * dates_dev, dates_dev)
                total = looked[n]
                if c > 0:
                    total = total + floor_ref[at]
                if last:
                    total = lax.rsqrt(jnp.maximum(total, 1.0))
                floor_ref[at] = total

        powers([date] + sources)
        s_copies[c].wait_recv()
        for k in range(len(sources)):
            r_copies[c, k].wait_recv()
        powers([sibling] + across)

        batch = largest_divisor(slots, max(1, BATCH_ROWS // blocks))

        def pair_body(n, carry):
            sums, scales = [], []
            for g in range(batch):
                p = n * batch + g
                i, j = pairs_ref[0, p], pairs_ref[1, p]
                first, second = panel[i].astype(F32), panel[j].astype(F32)
                ra, ia, rb, ib = first[:, :wc], first[:, wc:], second[:, :wc], second[:, wc:]
                sums.append(row_sum(ra * rb + ia * ib))
                sums.append(row_sum(ia * rb - ra * ib))
                if last:
                    scales.append(floor_ref[i] * floor_ref[j])
            looked = col_sum(jnp.concatenate(sums, axis=0), table).reshape(batch, 2, looks, 128)
            at = pl.ds(n * batch, batch)
            if c > 0:
                looked = looked + out_ref[at]
            if last:
                looked = looked * jnp.stack(scales)[:, None]
            out_ref[at] = looked
            return carry

        lax.fori_loop(0, slots // batch, pair_body, 0, unroll=True)

    for c in range(CHUNKS):
        stage_send(c)
    for c in range(CHUNKS):
        stage_z(c)
    for c in range(CHUNKS):
        stage_own(c)
    fetches[2].wait()
    for c in range(CHUNKS):
        stage_forward(c)
        if c > 0:
            stage_looks(c - 1)
    stage_looks(CHUNKS - 1)
    for copies in (z_copies, d_copies, s_copies, r_copies):
        for copy in copies.values():
            copy.wait_send()


def on_device(slc, footprint, valid_rows, pair_dates):
    groups, n_date = lax.axis_size("space"), lax.axis_size("date")
    dates_dev, blocks, twice = slc.shape
    width = twice // 2
    cap = blocks // groups
    slots = pair_dates.shape[0]
    looks = blocks // 4
    wc = width // CHUNKS
    others = n_date // 2 - 1
    sem = pltpu.SemaphoreType.DMA
    cfg = (groups, n_date, dates_dev, blocks, width, cap, slots)
    far = functools.partial(pltpu.with_memory_space_constraint, memory_space=pltpu.HBM)
    hbm, smem = pl.BlockSpec(memory_space=pltpu.HBM), pl.BlockSpec(memory_space=pltpu.SMEM)
    result = pl.pallas_call(
        functools.partial(kernel, cfg),
        out_shape=jax.ShapeDtypeStruct((slots, 2, looks, 128), F32),
        in_specs=[hbm, hbm, smem, hbm],
        out_specs=pl.BlockSpec(memory_space=pltpu.VMEM),
        scratch_shapes=[pltpu.VMEM((groups - 1, dates_dev * cap, 2 * wc), BF16)] * CHUNKS
        + [pltpu.VMEM((n_date, groups, dates_dev * cap, 2 * wc), BF16)] * CHUNKS
        + [pltpu.VMEM((n_date * dates_dev, blocks, 2 * wc), BF16)] * CHUNKS
        + [
            pltpu.VMEM((n_date * dates_dev, looks, 128), F32),
            sem((CHUNKS, groups - 1)),
            sem((CHUNKS, groups - 1)),
            sem((CHUNKS, 2, others)),
            sem((CHUNKS, 2, others)),
            sem((CHUNKS, others)),
            sem((CHUNKS, others)),
            sem((CHUNKS,)),
            sem((CHUNKS,)),
            pltpu.VMEM((dates_dev * blocks, twice), BF16),
            pltpu.VMEM(footprint.shape[::-1], jnp.int32),
            pltpu.SMEM(pair_dates.shape[::-1], jnp.int32),
            sem((3,)),
        ],
        compiler_params=pltpu.CompilerParams(
            collective_id=0, has_side_effects=True, vmem_limit_bytes=40 * 1024 * 1024
        ),
    )(far(slc.reshape(dates_dev * blocks, twice)), far(footprint.T), valid_rows, far(pair_dates.T))
    return result[:, None]


def solution(mesh):
    in_specs = (P("date", "space", None), P(), P("space"), P("date", None))
    out_specs = P("date", "space", None, None, None)
    return jax.shard_map(
        on_device, mesh=mesh, in_specs=in_specs, out_specs=out_specs, check_vma=False
    )
```

```python
import functools

import jax
import jax.numpy as jnp
from jax import lax
from jax.experimental import pallas as pl
from jax.experimental.pallas import tpu as pltpu
from jax.sharding import PartitionSpec as P

CHUNKS = 4
BATCH_ROWS = 1056
MESH = pl.DeviceIdType.MESH
F32, BF16 = jnp.float32, jnp.bfloat16


def largest_divisor(count, most):
    return max(g for g in range(1, most + 1) if count % g == 0)


def partners(date, n_date):
    chips = n_date // 2
    chip, core = date // 2, date % 2
    sibling = chip * 2 + (1 - core)
    if chips == 4:
        x, y = chip % 2, chip // 2
        near = [y * 2 + 1 - x, (1 - y) * 2 + x, (1 - y) * 2 + 1 - x]
        others = [near[k] * 2 + core for k in (2, 0, 1)]
        return sibling, others, others
    targets = [lax.rem(chip + k, chips) * 2 + core for k in range(1, chips)]
    sources = [lax.rem(chip + chips - k, chips) * 2 + core for k in range(1, chips)]
    return sibling, targets, sources


def tables(cfg, foot, valid, own):
    groups, n_date, dates_dev, blocks, width, cap, slots = cfg
    total, looks, lane = groups * blocks, blocks // 4, 128
    tile, row = foot[0:1], foot[1:2]
    tile_step = jnp.where(tile < 0, -1, lax.rem(tile - own + groups, groups))

    def index(shape, dim):
        return lax.broadcasted_iota(jnp.int32, shape, dim)

    def ones(mask):
        return mask.astype(F32).astype(BF16)

    earlier = (index((lane, lane), 0) < index((lane, lane), 1)) & (
        lax.div(index((lane, lane), 0), blocks) == lax.div(index((lane, lane), 1), blocks)
    )
    ranks = []
    for at in range(0, total, lane):
        hot = index((max(groups, 8), lane), 0) == tile[:, at : at + lane]
        count = jnp.dot(ones(hot), ones(earlier), preferred_element_type=F32)
        ranks.append(jnp.sum(jnp.where(hot, count, 0.0), axis=0, keepdims=True))
    rank = jnp.concatenate(ranks, axis=1).astype(jnp.int32)

    n_slot, n_place = groups * dates_dev * cap, dates_dev * blocks
    slot = index((n_slot, total), 0)
    slot_group, slot_rank = lax.div(slot, dates_dev * cap), lax.rem(slot, cap)
    slot_date = lax.rem(lax.div(index((n_slot, n_place), 0), cap), dates_dev)
    fits = slot_rank == rank
    leaves = ones(fits & (slot_group == tile_step))
    held = ones(index((total, n_place), 0) == own * blocks + lax.rem(index((total, n_place), 1), blocks))
    select = jnp.dot(leaves, held, preferred_element_type=F32)
    select = jnp.where(slot_date == lax.div(index((n_slot, n_place), 1), blocks), select, 0.0)

    place_at = lax.rem(row, 4) * looks + lax.div(row, 4)
    place_at = jnp.where((tile == own) & (row < valid), place_at, -1)
    lands = ones(lax.rem(index((n_place, total), 0), blocks) == place_at)
    from_step = lax.rem(lax.div(index((n_slot, total), 1), blocks) - own + groups, groups)
    comes = ones(fits & (slot_group == from_step))
    place = lax.dot_general(lands, comes, (((1,), (1,)), ((), ())), preferred_element_type=F32)
    from_date = lax.rem(lax.div(index((n_place, n_slot), 1), cap), dates_dev)
    place = jnp.where(from_date == lax.div(index((n_place, n_slot), 0), blocks), place, 0.0)
    return select.astype(BF16), place.astype(BF16)


def kernel(cfg, slc_hbm, foot_hbm, valid_ref, pairs_hbm, out_ref, *scratch):
    groups, n_date, dates_dev, blocks, width, cap, slots = cfg
    out_bufs, slot_bufs = scratch[:CHUNKS], scratch[CHUNKS : 2 * CHUNKS]
    panels = scratch[2 * CHUNKS : 3 * CHUNKS]
    rest = scratch[3 * CHUNKS :]
    floor_ref, z_send, z_recv, d_send, d_recv, f_send, f_recv, c_send, c_recv = rest[:9]
    slc_ref, foot_ref, pairs_ref, in_sem = rest[9:]
    wc = width // CHUNKS
    looks = blocks // 4
    dates = n_date * dates_dev
    own, date = lax.axis_index("space"), lax.axis_index("date")
    sibling, targets, sources = partners(date, n_date)
    across = partners(sibling, n_date)[2]
    peers = [lax.rem(own + k, groups) for k in range(1, groups)]

    barrier = pltpu.get_barrier_semaphore()
    for peer in peers:
        pl.semaphore_signal(barrier, inc=1, device_id={"space": peer}, device_id_type=MESH)
    for target in targets + [sibling]:
        pl.semaphore_signal(barrier, inc=1, device_id={"date": target}, device_id_type=MESH)

    fetches = [
        pltpu.make_async_copy(src, dst, in_sem.at[k])
        for k, (src, dst) in enumerate([(foot_hbm, foot_ref), (slc_hbm, slc_ref), (pairs_hbm, pairs_ref)])
    ]
    for fetch in fetches:
        fetch.start()
    fetches[0].wait()
    select, place = tables(cfg, foot_ref[...], valid_ref[0], own)
    fetches[1].wait()

    def gather_rows(c):
        for part in range(2):
            cols = slice(part * width + c * wc, part * width + c * wc + wc)
            half = slice(part * wc, (part + 1) * wc)
            rows = jnp.dot(select, slc_ref[:, cols], preferred_element_type=F32).astype(BF16)
            rows = rows.reshape(groups, dates_dev * cap, wc)
            slot_bufs[c][date, 0, :, half] = rows[0]
            out_bufs[c][:, :, half] = rows[1:]

    def z_copy(c, k):
        return pltpu.make_async_remote_copy(
            src_ref=out_bufs[c].at[k],
            dst_ref=slot_bufs[c].at[date, groups - 1 - k],
            send_sem=z_send.at[c, k],
            recv_sem=z_recv.at[c, k],
            device_id={"space": peers[k]},
            device_id_type=MESH,
        )

    def slot_copy(c, part, target, send_sem, recv_sem):
        steps = pl.ds(0, 1) if part == 0 else pl.ds(1, groups - 1)
        block = slot_bufs[c].at[date, steps]
        return pltpu.make_async_remote_copy(
            src_ref=block,
            dst_ref=block,
            send_sem=send_sem,
            recv_sem=recv_sem,
            device_id={"date": target},
            device_id_type=MESH,
        )

    z_copies, d_copies, s_copies, r_copies = {}, {}, {}, {}

    def send(c, part):
        for k, target in enumerate(targets):
            d_copies[c, part, k] = slot_copy(c, part, target, d_send.at[c, part, k], d_recv.at[c, part, k])
            d_copies[c, part, k].start()

    def panel_copy(c, source, send_sem, recv_sem):
        block = panels[c].at[pl.ds(source * dates_dev, dates_dev)]
        return pltpu.make_async_remote_copy(
            src_ref=block,
            dst_ref=block,
            send_sem=send_sem,
            recv_sem=recv_sem,
            device_id={"date": sibling},
            device_id_type=MESH,
        )

    def fill(c, source):
        rows = slot_bufs[c][source].reshape(groups * dates_dev * cap, 2 * wc)
        tile = jnp.dot(place, rows, preferred_element_type=F32).astype(BF16)
        panels[c][pl.ds(source * dates_dev, dates_dev)] = tile.reshape(dates_dev, blocks, 2 * wc)

    def stage_send(c):
        gather_rows(c)
        if c == 0:
            pl.semaphore_wait(barrier, len(peers) + len(targets) + 1)
        for k in range(len(peers)):
            z_copies[c, k] = z_copy(c, k)
            z_copies[c, k].start()
        send(c, 0)

    def stage_z(c):
        for k in range(len(peers)):
            z_copies[c, k].wait_recv()
        send(c, 1)

    def stage_own(c):
        fill(c, date)
        s_copies[c] = panel_copy(c, date, c_send.at[c], c_recv.at[c])
        s_copies[c].start()

    def stage_forward(c):
        for k in range(len(sources)):
            for part in range(2):
                d_copies[c, part, k].wait_recv()
        for k in range(len(sources)):
            fill(c, sources[k])
        for k in range(len(sources)):
            r_copies[c, k] = panel_copy(c, sources[k], f_send.at[c, k], f_recv.at[c, k])
            r_copies[c, k].start()

    def row_sum(field):
        quads = field.reshape(4, looks, field.shape[1])
        last = lax.broadcasted_iota(jnp.int32, quads[0].shape, 0) == looks - 1
        below = jnp.where(last, 0.0, pltpu.roll(quads[0], looks - 1, 0))
        return (quads[0] + quads[1]) + (quads[2] + quads[3]) + below

    def col_sum(rows, table):
        return jnp.dot(rows.astype(BF16), table, preferred_element_type=F32)

    def stage_looks(c):
        panel = panels[c]
        col_in = lax.broadcasted_iota(jnp.int32, (wc, 128), 0) + c * wc
        col_out = lax.broadcasted_iota(jnp.int32, (wc, 128), 1)
        table = (jnp.abs(col_in - 4 * col_out - 2) <= 5).astype(F32).astype(BF16)
        last = c == CHUNKS - 1

        def powers(blocks_of):
            sums = []
            for source in blocks_of:
                for d in range(dates_dev):
                    rows = panel[source * dates_dev + d].astype(F32)
                    real, imag = rows[:, :wc], rows[:, wc:]
                    sums.append(row_sum(real * real + imag * imag))
            looked = col_sum(jnp.concatenate(sums, axis=0), table)
            looked = looked.reshape(len(blocks_of), dates_dev, looks, 128)
            for n, source in enumerate(blocks_of):
                at = pl.ds(source * dates_dev, dates_dev)
                total = looked[n]
                if c > 0:
                    total = total + floor_ref[at]
                if last:
                    total = lax.rsqrt(jnp.maximum(total, 1.0))
                floor_ref[at] = total

        powers([date] + sources)
        s_copies[c].wait_recv()
        for k in range(len(sources)):
            r_copies[c, k].wait_recv()
        powers([sibling] + across)

        batch = largest_divisor(slots, max(1, BATCH_ROWS // blocks))

        def pair_body(n, carry):
            sums, scales = [], []
            for g in range(batch):
                p = n * batch + g
                i, j = pairs_ref[0, p], pairs_ref[1, p]
                first, second = panel[i].astype(F32), panel[j].astype(F32)
                ra, ia, rb, ib = first[:, :wc], first[:, wc:], second[:, :wc], second[:, wc:]
                sums.append(row_sum(ra * rb + ia * ib))
                sums.append(row_sum(ia * rb - ra * ib))
                if last:
                    scales.append(floor_ref[i] * floor_ref[j])
            looked = col_sum(jnp.concatenate(sums, axis=0), table).reshape(batch, 2, looks, 128)
            at = pl.ds(n * batch, batch)
            if c > 0:
                looked = looked + out_ref[at]
            if last:
                looked = looked * jnp.stack(scales)[:, None]
            out_ref[at] = looked
            return carry

        lax.fori_loop(0, slots // batch, pair_body, 0, unroll=True)

    for c in range(CHUNKS):
        stage_send(c)
    for c in range(CHUNKS):
        stage_z(c)
        if c > 0:
            stage_own(c - 1)
    stage_own(CHUNKS - 1)
    fetches[2].wait()
    for c in range(CHUNKS):
        stage_forward(c)
        if c > 0:
            stage_looks(c - 1)
    kinds = (z_copies, d_copies, s_copies, r_copies)
    early, late = [], []
    for copies in kinds:
        for at, copy in copies.items():
            chunk = at if copies is s_copies else at[0]
            (late if chunk == CHUNKS - 1 and copies is not z_copies else early).append(copy)
    for copy in early:
        copy.wait_send()
    stage_looks(CHUNKS - 1)
    for copy in late:
        copy.wait_send()


def on_device(slc, footprint, valid_rows, pair_dates):
    groups, n_date = lax.axis_size("space"), lax.axis_size("date")
    dates_dev, blocks, twice = slc.shape
    width = twice // 2
    cap = blocks // groups
    slots = pair_dates.shape[0]
    looks = blocks // 4
    wc = width // CHUNKS
    others = n_date // 2 - 1
    sem = pltpu.SemaphoreType.DMA
    cfg = (groups, n_date, dates_dev, blocks, width, cap, slots)
    far = functools.partial(pltpu.with_memory_space_constraint, memory_space=pltpu.HBM)
    hbm, smem = pl.BlockSpec(memory_space=pltpu.HBM), pl.BlockSpec(memory_space=pltpu.SMEM)
    result = pl.pallas_call(
        functools.partial(kernel, cfg),
        out_shape=jax.ShapeDtypeStruct((slots, 2, looks, 128), F32),
        in_specs=[hbm, hbm, smem, hbm],
        out_specs=pl.BlockSpec(memory_space=pltpu.VMEM),
        scratch_shapes=[pltpu.VMEM((groups - 1, dates_dev * cap, 2 * wc), BF16)] * CHUNKS
        + [pltpu.VMEM((n_date, groups, dates_dev * cap, 2 * wc), BF16)] * CHUNKS
        + [pltpu.VMEM((n_date * dates_dev, blocks, 2 * wc), BF16)] * CHUNKS
        + [
            pltpu.VMEM((n_date * dates_dev, looks, 128), F32),
            sem((CHUNKS, groups - 1)),
            sem((CHUNKS, groups - 1)),
            sem((CHUNKS, 2, others)),
            sem((CHUNKS, 2, others)),
            sem((CHUNKS, others)),
            sem((CHUNKS, others)),
            sem((CHUNKS,)),
            sem((CHUNKS,)),
            pltpu.VMEM((dates_dev * blocks, twice), BF16),
            pltpu.VMEM(footprint.shape[::-1], jnp.int32),
            pltpu.SMEM(pair_dates.shape[::-1], jnp.int32),
            sem((3,)),
        ],
        compiler_params=pltpu.CompilerParams(
            collective_id=0, has_side_effects=True, vmem_limit_bytes=40 * 1024 * 1024
        ),
    )(far(slc.reshape(dates_dev * blocks, twice)), far(footprint.T), valid_rows, far(pair_dates.T))
    return result[:, None]


def solution(mesh):
    in_specs = (P("date", "space", None), P(), P("space"), P("date", None))
    out_specs = P("date", "space", None, None, None)
    return jax.shard_map(
        on_device, mesh=mesh, in_specs=in_specs, out_specs=out_specs, check_vma=False
    )
```
